512 devices in a mesh: video: 128 (over z_lo, x, y), head: 4 (over z_hi, core).
Axes of the slice: x: 4, y: 4, z: 16 (z_hi: 2, z_lo: 8; z = z_hi * 8 + z_lo), core: 2. Of those that a mesh axis runs over, the one named last changes fastest.
Arguments:
- qkv: bfloat16 [128, 768, 3, 1536], P('video', 'head'), may hold values from -50 to 50
- tile_masks: int32 [128, 2, 6, 6], replicated, may hold values 0 or 1
Outputs:
- attended: bfloat16 [128, 768, 1536], P('video', 'head')
The draws below stay inside these ranges and needn't reach their ends.
All inputs are finite; a program needn't handle non-finite values.
Results may differ from the reference program's by a relative error of at most 0.0036.
Values may be sent and summed in bfloat16 or wider, within the bound.
A program may use at most 64 MiB of HBM per device.

```python
import jax
import jax.numpy as jnp
from jax import lax

D = 1536
HEADS = 16
DH = 96
TOK = 768
TILE = 128
TILES = 6
VIDEOS = 128


def draw_qkv(key, part):
    key = jax.random.fold_in(key, 11)
    keys = jax.random.split(key, 1)
    shape = (VIDEOS, TOK, 3, D)
    base = jnp.clip(jax.random.normal(keys[0], shape, jnp.float32), -6.0, 6.0)
    query = base[:, :, 0] * 2.0
    keyed = base[:, :, 1]
    valued = base[:, :, 2]
    return jnp.stack([query, keyed, valued], axis=2).astype(jnp.bfloat16)


def touch_ends(values, rng, least, top_value):
    longest = values.shape.index(max(values.shape))
    spots = []
    for shift in (0, 1):
        where = [jax.random.randint(jax.random.fold_in(rng, axis), (), 0, length) for axis, length in enumerate(values.shape)]
        where[longest] = (where[longest] + shift) % values.shape[longest]
        spots.append(tuple(where))
    return values.at[spots[0]].set(least).at[spots[1]].set(top_value)


def setup_inputs(seed: int = 0) -> dict:
    splits = jax.random.split(jax.random.key(seed), 3)
    return {
        "qkv": draw_qkv(jax.random.fold_in(splits[2], 71), 0),
        "tile_masks": touch_ends((jax.random.randint(splits[1], (VIDEOS, 2, TILES, TILES), 0, 2) < 1).astype(jnp.int32), jax.random.fold_in(splits[1], 1), 0, 1),
    }


def expand_tiles(tiles):
    return jnp.repeat(jnp.repeat(tiles, TILE, axis=0), TILE, axis=1) > 0


def one_video(index, qkv, tile_masks):
    offsets = [0, 1, 2, -1, -2]
    picks = [(index + VIDEOS + off) % VIDEOS for off in offsets]
    keys = jnp.concatenate([qkv[p, :, 1] for p in picks], axis=0)
    values = jnp.concatenate([qkv[p, :, 2] for p in picks], axis=0)
    ones = jnp.ones((TILES, TILES), jnp.int32)
    tiles = jnp.concatenate([ones, tile_masks[index, 0], tile_masks[index, 1],
                             tile_masks[picks[3], 0].T, tile_masks[picks[4], 1].T], axis=1)
    visible = expand_tiles(tiles)
    query = qkv[index, :, 0].reshape(TOK, HEADS, DH).astype(jnp.float32)
    keyed = keys.reshape(5 * TOK, HEADS, DH).astype(jnp.float32)
    valued = values.reshape(5 * TOK, HEADS, DH).astype(jnp.float32)
    scores = jnp.einsum("qhd,khd->hqk", query, keyed) * (DH ** -0.5)
    scores = jnp.where(visible[None], scores, -jnp.inf)
    top = jnp.max(scores, axis=-1, keepdims=True)
    weights = jnp.exp(scores - top)
    total = jnp.sum(weights, axis=-1, keepdims=True)
    rounded = lax.optimization_barrier(weights.astype(jnp.bfloat16)).astype(jnp.float32)
    summed = jnp.einsum("hqk,khd->qhd", rounded, valued)
    result = summed / jnp.moveaxis(total, 0, 1)
    return result.reshape(TOK, D).astype(jnp.bfloat16)


def reference(qkv, tile_masks):
    indices = jnp.arange(VIDEOS, dtype=jnp.int32)
    return lax.map(lambda index: one_video(index, qkv, tile_masks), indices)
```

```python
import functools

import jax
import jax.numpy as jnp
from jax import lax
from jax.experimental import pallas as pl
from jax.experimental.pallas import tpu as pltpu
from jax.sharding import PartitionSpec as P

MESH = pl.DeviceIdType.MESH
DH = 96
TILE = 128
ROWS = 192
TOK = 768
TILES = TOK // TILE
WIDTH = 384
PAIR = 256
SUB = 64
KEYS = 256
SCALE = DH ** (-0.5) * 1.4426950408889634
OWN, MATE, FAR, CROSS = 3, 2, 0, 1


def kernel(x_ref, masks_ref, out_ref, kv, q, obuf, scores, top, total, acc, masks, seen, bias,
           local_sem, ex_send, ex_recv, nb_send, nb_recv, fw_send, fw_recv, ret_send, ret_recv):
    video = lax.axis_index("video")
    group = lax.axis_index("head")
    videos = lax.axis_size("video")
    half, core = group // 2, group % 2
    up = lax.rem(video + 1, videos)
    down = lax.rem(video + videos - 1, videos)

    def group_of(who):
        if isinstance(who, int):
            far, crossed = int(who in (FAR, CROSS)), int(who in (CROSS, MATE))
        else:
            far, crossed = 1 - who // 2, lax.rem(lax.rem(who, 2) + who // 2, 2)
            crossed = jnp.where(who < 2, lax.rem(who, 2), 1 - lax.rem(who, 2))
        return lax.rem(half + far, 2) * 2 + lax.rem(core + crossed, 2)

    def device(who):
        return {"video": video, "head": group_of(who)}

    def along(direction):
        return {"video": (down, up)[direction], "head": group}

    def rows(who):
        return pl.ds(pl.multiple_of(group_of(who) * ROWS, SUB), ROWS)

    def columns(who):
        return pl.ds(pl.multiple_of(group_of(who) * WIDTH, 128), WIDTH)

    here = rows(OWN)
    copies = []

    own_kv = pltpu.make_async_copy(x_ref.at[pl.ds(1, 2), :, columns(OWN)], kv.at[0, :, here], local_sem.at[0])
    own_q = pltpu.make_async_copy(x_ref.at[0, :, columns(OWN)], q.at[here], local_sem.at[1])
    get_masks = pltpu.make_async_copy(masks_ref, masks, local_sem.at[2])
    barrier = pltpu.get_barrier_semaphore()
    for who in (FAR, CROSS, MATE):
        pl.semaphore_signal(barrier, inc=1, device_id=device(who), device_id_type=MESH)
    for direction in (0, 1):
        pl.semaphore_signal(barrier, inc=1, device_id=along(direction), device_id_type=MESH)
    get_masks.start()
    own_kv.start()
    own_q.start()
    pl.semaphore_wait(barrier, 5)

    def remote(src, dst, send, recv, to):
        return pltpu.make_async_remote_copy(
            src_ref=src, dst_ref=dst, send_sem=send, recv_sem=recv, device_id=to, device_id_type=MESH)

    def give_kv(who):
        return remote(x_ref.at[pl.ds(1, 2), :, columns(who)], kv.at[0, :, here], ex_send.at[0, who], ex_recv.at[0, who], device(who))

    def give_q(who):
        return remote(x_ref.at[0, :, columns(who)], q.at[here], ex_send.at[1, who], ex_recv.at[1, who], device(who))

    def take_kv(who):
        return remote(x_ref.at[pl.ds(1, 2), :, columns(who)], kv.at[0, :, rows(who)], ex_send.at[0, who], ex_recv.at[0, who], device(who))

    def take_q(who):
        return remote(x_ref.at[0, :, columns(OWN)], q.at[rows(who)], ex_send.at[1, who], ex_recv.at[1, who], device(who))

    first, second = (1, 3), (2, 4)

    def to_neighbour(who, direction):
        src = x_ref.at[pl.ds(1, 2), :, columns(OWN)] if who == OWN else kv.at[0, :, rows(who)]
        return remote(src, kv.at[first[direction], :, rows(who)], nb_send.at[direction, who], nb_recv.at[direction, who], along(direction))

    def pass_on(who, direction):
        return remote(kv.at[first[direction], :, rows(who)], kv.at[second[direction], :, rows(who)],
                      fw_send.at[direction, who], fw_recv.at[direction, who], along(direction))

    def start(copy):
        copy.start()
        copies.append(copy)

    start(give_kv(MATE))
    for direction in (0, 1):
        start(to_neighbour(OWN, direction))
    start(give_kv(FAR))
    start(give_kv(CROSS))
    start(give_q(FAR))
    start(give_q(CROSS))
    start(give_q(MATE))

    get_masks.wait()
    lane = lax.broadcasted_iota(jnp.int32, (TILES, TILES, 2, 128), 3)
    for back in (0, 1, 2):
        who = lax.rem(video + videos - back, videos)
        value = jnp.sum(jnp.where(lane == who, masks[...].astype(jnp.float32), 0.0), axis=3, keepdims=True)
        seen[back] = jnp.broadcast_to(jnp.where(value > 0.5, 0.0, -jnp.inf), (TILES, TILES, 2, 128))
    bias[0] = jnp.zeros((TILES, TILES, 128), jnp.float32)
    for i in range(TILES):
        bias[1, i] = seen[0, i, :, 0, :]
        bias[2, i] = seen[0, i, :, 1, :]
        bias[3, i] = seen[1, :, i, 0, :]
        bias[4, i] = seen[2, :, i, 1, :]

    def hand_out(who):
        take_kv(who).wait_recv()
        for direction in (0, 1):
            start(to_neighbour(who, direction))

    def hand_on(who):
        for direction in (0, 1):
            to_neighbour(who, direction).wait_recv()
            start(pass_on(who, direction))

    hand_out(MATE)
    hand_on(OWN)
    hand_on(MATE)
    hand_out(FAR)
    hand_on(FAR)
    hand_out(CROSS)
    hand_on(CROSS)
    own_kv.wait()
    own_q.wait()
    for who in (OWN, MATE, FAR, CROSS):
        for direction in (0, 1):
            pass_on(who, direction).wait_recv()

    stacked = 2 * ROWS

    def attend(block, slot):
        for pair in (0, 1):
            lanes = pl.ds(128 * pair, PAIR)
            base = (0, 64)[pair]
            at = lax.broadcasted_iota(jnp.int32, (ROWS, PAIR), 1)
            qp = q[pl.ds(pl.multiple_of(block * ROWS, SUB), ROWS), lanes]
            heads = [jnp.where((at >= base + DH * n) & (at < base + DH * (n + 1)), qp, jnp.zeros_like(qp)) for n in (0, 1)]
            qs = jnp.concatenate(heads, axis=0)
            top[...] = jnp.full((stacked, 128), -jnp.inf, jnp.float32)

            def score(s, _):
                for kb in range(TOK // KEYS):
                    k = kv[s, 0, pl.ds(kb * KEYS, KEYS), lanes]
                    sc = lax.dot_general(qs, k, (((1,), (1,)), ((), ())), preferred_element_type=jnp.float32)
                    cols = []
                    for kt in range(KEYS // 128):
                        parts = []
                        for sub in range(ROWS // SUB):
                            tile = (block * (ROWS // SUB) + sub) // (TILE // SUB)
                            row = bias[s, tile, pl.ds(kb * (KEYS // 128) + kt, 1), :]
                            parts.append(jnp.broadcast_to(row, (SUB, 128)))
                        cols.append(jnp.concatenate(parts * 2, axis=0))
                    sc = sc + jnp.concatenate(cols, axis=1)
                    scores[s * (TOK // KEYS) + kb] = sc
                    top[...] = jnp.maximum(top[...], jnp.maximum(sc[:, :128], sc[:, 128:]))
                return 0

            lax.fori_loop(0, 5, score, 0)
            top[...] = jnp.broadcast_to(jnp.max(top[...], axis=1, keepdims=True), (stacked, 128))
            total[...] = jnp.zeros((stacked, 128), jnp.float32)
            acc[...] = jnp.zeros((stacked, PAIR), jnp.float32)

            def weigh(s, _):
                ws = []
                highest = top[...]
                both = jnp.concatenate([highest, highest], axis=1)
                for kb in range(TOK // KEYS):
                    w = jnp.exp2((scores[s * (TOK // KEYS) + kb] - both) * SCALE)
                    total[...] += w[:, :128] + w[:, 128:]
                    ws.append(w.astype(jnp.bfloat16))
                acc[...] += jnp.dot(jnp.concatenate(ws, axis=1), kv[s, 1, :, lanes], preferred_element_type=jnp.float32)
                return 0

            lax.fori_loop(0, 5, weigh, 0)
            o = acc[...] / jnp.sum(total[...], axis=1, keepdims=True)
            o = jnp.where(at < base + DH, o[:ROWS], o[ROWS:])
            if pair == 1:
                o = jnp.concatenate([
                    jnp.where(at[:, :128] < 64, obuf[slot, :, pl.ds(128, 128)].astype(jnp.float32), o[:, :128]),
                    o[:, 128:]], axis=1)
            obuf[slot, :, lanes] = o.astype(jnp.bfloat16)

    def give_back(who):
        return remote(obuf.at[who], out_ref.at[:, columns(OWN)], ret_send.at[who], ret_recv.at[who], device(who))

    def take_back(who):
        return remote(obuf.at[who], out_ref.at[:, columns(who)], ret_send.at[who], ret_recv.at[who], device(who))

    keep = pltpu.make_async_copy(obuf.at[OWN], out_ref.at[:, columns(OWN)], local_sem.at[3])

    def piece(who, _):
        for other in (FAR, CROSS, MATE):
            pl.when(who == other)(lambda other=other: take_q(other).wait_recv())
        attend(group_of(who), who)
        for other in (FAR, CROSS, MATE):
            pl.when(who == other)(lambda other=other: give_back(other).start())
        pl.when(who == OWN)(keep.start)
        return 0

    lax.fori_loop(0, 4, piece, 0)

    for who in (FAR, CROSS, MATE):
        take_back(who).wait_recv()
        give_back(who).wait_send()
    keep.wait()
    for copy in copies:
        copy.wait_send()


def body(qkv, tile_masks):
    x = jnp.transpose(qkv[0], (1, 0, 2))
    masks = jnp.transpose(tile_masks, (2, 3, 1, 0))
    dma = pltpu.SemaphoreType.DMA
    stacked = 2 * ROWS
    out = pl.pallas_call(
        kernel,
        out_shape=jax.ShapeDtypeStruct((ROWS, x.shape[2]), jnp.bfloat16),
        in_specs=[pl.BlockSpec(memory_space=pl.ANY)] * 2,
        out_specs=pl.BlockSpec(memory_space=pl.ANY),
        scratch_shapes=[
            pltpu.VMEM((5, 2, TOK, WIDTH), jnp.bfloat16),
            pltpu.VMEM((TOK, WIDTH), jnp.bfloat16),
            pltpu.VMEM((4, ROWS, WIDTH), jnp.bfloat16),
            pltpu.VMEM((5 * TOK // KEYS, stacked, KEYS), jnp.float32),
            pltpu.VMEM((stacked, 128), jnp.float32),
            pltpu.VMEM((stacked, 128), jnp.float32),
            pltpu.VMEM((stacked, PAIR), jnp.float32),
            pltpu.VMEM(masks.shape, jnp.int32),
            pltpu.VMEM((3, TILES, TILES, 2, 128), jnp.float32),
            pltpu.VMEM((5, TILES, TILES, 128), jnp.float32),
            dma((4,)),
            dma((2, 3)), dma((2, 3)),
            dma((2, 4)), dma((2, 4)),
            dma((2, 4)), dma((2, 4)),
            dma((3,)), dma((3,)),
        ],
        compiler_params=pltpu.CompilerParams(collective_id=1, has_side_effects=True, vmem_limit_bytes=48 * 2**20),
        name="orbit_attention",
    )(x, masks)
    return out[None]


def solution(mesh):
    placed = (P("video", "head", None, None), P())
    return jax.shard_map(
        body, mesh=mesh, in_specs=placed, out_specs=P("video", "head", None), check_vma=False
    )
```

```python
import jax
import jax.numpy as jnp
from jax import lax
from jax.experimental import pallas as pl
from jax.experimental.pallas import tpu as pltpu
from jax.sharding import PartitionSpec as P

MESH = pl.DeviceIdType.MESH
DH = 96
TILE = 128
ROWS = 192
HALF = 384
TILES = 6
HTILES = HALF // TILE
WIDTH = 384
PAIR = 256
KEYS = 256
SPAN = 2048
STEPS = 4
SCALE = DH ** (-0.5) * 1.4426950408889634
OWN, MATE = 0, 1
FAR, CROSS = 0, 1
PLANE = 16
SIDE = 4
EDGE = (0, PLANE - 1)


def kernel(x_ref, masks_ref, out_ref, kv, q, part, partial_in, near, fin, stat, stat_out, stat_in, scores, top, total, acc,
           masks, seen, bias, held, local_sem, mate_send, mate_recv, far_send, far_recv, nb_send, nb_recv, fw_send, fw_recv,
           hop_send, hop_recv, back_send, back_recv, fin_send, fin_recv):
    video = lax.axis_index("video")
    group = lax.axis_index("head")
    videos = lax.axis_size("video")
    half, core = group // 2, lax.rem(group, 2)
    other_half, other_core = 1 - half, 1 - core
    up = lax.rem(video + 1, videos)
    down = lax.rem(video + videos - 1, videos)
    planes = videos // PLANE
    plane, column = video // PLANE, lax.rem(video, PLANE)
    across, row = column // SIDE, lax.rem(column, SIDE)

    mate = {"video": video, "head": half * 2 + other_core}
    far = ({"video": video, "head": other_half * 2 + core}, {"video": video, "head": other_half * 2 + other_core})

    def along(direction):
        return {"video": (down, up)[direction], "head": group}

    def at_column(level, col):
        return {"video": lax.rem(level + planes, planes) * PLANE + col, "head": group}

    def columns(of_core, n):
        return pl.ds(pl.multiple_of((of_core * 2 + n) * WIDTH, 128), WIDTH)

    def rows(of_core, slot=0):
        return pl.ds(pl.multiple_of(slot * HALF + of_core * ROWS, 64), ROWS)

    both = pl.ds(1, 2)
    core_of = (core, other_core)

    def remote(src, dst, send, recv, to):
        return pltpu.make_async_remote_copy(
            src_ref=src, dst_ref=dst, send_sem=send, recv_sem=recv, device_id=to, device_id_type=MESH)

    copies = []

    def start(copy):
        copy.start()
        copies.append(copy)

    get_masks = pltpu.make_async_copy(masks_ref, masks, local_sem.at[0])
    own_kv = [pltpu.make_async_copy(x_ref.at[both, :, columns(core, n)], kv.at[n, :, rows(core)], local_sem.at[1 + n]) for n in (0, 1)]
    own_q = [pltpu.make_async_copy(x_ref.at[0, :, columns(core, n)], q.at[2 + n, rows(core)], local_sem.at[3 + n]) for n in (0, 1)]
    get_masks.start()
    for copy in own_kv + own_q:
        copy.start()

    barrier = pltpu.get_barrier_semaphore()

    def greet(to):
        pl.semaphore_signal(barrier, inc=1, device_id=to, device_id_type=MESH)

    for to in (*far, mate, along(0), along(1)):
        greet(to)

    relays_up = (row == SIDE - 1) & (across != SIDE - 1)
    relays_down = (row == 0) & (across != 0)
    relaying = relays_up | relays_down
    expected = 5 + relaying.astype(jnp.int32)
    for direction, role in ((0, relays_down), (1, relays_up)):
        pl.when(role)(lambda direction=direction: greet(at_column(plane, EDGE[direction])))

        @pl.when(column == EDGE[1 - direction])
        def _():
            for place in range(SIDE):
                col = place * SIDE + EDGE[direction] % SIDE
                if col != EDGE[direction]:
                    greet(at_column(plane + (1, -1)[direction], col))

        expected += jnp.where(column == EDGE[direction], SIDE - 1, 0)

    pl.semaphore_wait(barrier, expected)

    def mate_kv(n):
        return remote(x_ref.at[both, :, columns(other_core, n)], kv.at[n, :, rows(core)], mate_send.at[0, n], mate_recv.at[0, n], mate)

    def mate_q(n):
        return remote(x_ref.at[0, :, columns(other_core, n)], q.at[2 + n, rows(core)], mate_send.at[1, n], mate_recv.at[1, n], mate)

    def far_q(n, which):
        return remote(x_ref.at[0, :, columns(core_of[which], n)], q.at[n, rows(core)], far_send.at[n, which], far_recv.at[n, which], far[which])

    slots = ((1, 3), (2, 4))

    def source_of(kind, n, block, direction):
        if kind:
            return kv.at[n, :, rows(core_of[block], slots[0][direction])]
        if block == OWN:
            return x_ref.at[both, :, columns(core, n)]
        return kv.at[n, :, rows(other_core)]

    def sems(kind, n, block, direction):
        send, recv = ((nb_send, nb_recv), (fw_send, fw_recv))[kind]
        return send.at[direction, n, block], recv.at[direction, n, block]

    def target_of(kind, n, block, direction):
        return kv.at[n, :, rows(core_of[block], slots[kind][direction])]

    def passing(kind, n, block, direction):
        return remote(source_of(kind, n, block, direction), target_of(kind, n, block, direction),
                      *sems(kind, n, block, direction), along(direction))

    def step(kind, n, block, direction):
        pl.when(column != EDGE[direction])(passing(kind, n, block, direction).start)

        @pl.when(column == EDGE[direction])
        def _():
            send, recv = sems(kind, n, block, direction)
            for which in (0, 1):
                place = block * 2 + which
                col = place * SIDE + EDGE[direction] % SIDE
                src = source_of(kind, n, block, direction).at[which]
                if col == EDGE[direction]:
                    remote(src, target_of(kind, n, block, direction).at[which], send, recv, along(direction)).start()
                else:
                    remote(src, held.at[kind, n], send, hop_recv.at[kind, n], at_column(plane, col)).start()

    def hop(kind, n):
        upward = relays_up.astype(jnp.int32)
        block, which = across // 2, lax.rem(across, 2)
        slot = jnp.where(relays_up, slots[kind][1], slots[kind][0])
        to_rows = rows(lax.rem(core + block, 2), slot)
        recv = (nb_recv, fw_recv)[kind].at[upward, n, block]
        to = at_column(plane + 2 * upward - 1, jnp.where(relays_up, EDGE[0], EDGE[1]))
        return remote(held.at[kind, n], kv.at[n, which, to_rows], hop_send.at[kind, n], recv, to)

    def relay(kind, n):
        @pl.when(relaying)
        def _():
            remote(held.at[kind, n], held.at[kind, n], hop_send.at[kind, n], hop_recv.at[kind, n], along(0)).wait_recv()
            hop(kind, n).start()

    def hand_on(n, direction):
        for block in (OWN, MATE):
            passing(0, n, block, direction).wait_recv()
            step(1, n, block, direction)

    def hand_on_early(n):
        pl.when(column != EDGE[1])(lambda: hand_on(n, 0))
        pl.when(column != EDGE[0])(lambda: hand_on(n, 1))

    def hand_on_late(n):
        pl.when(column == EDGE[1])(lambda: hand_on(n, 0))
        pl.when(column == EDGE[0])(lambda: hand_on(n, 1))

    def give(n, block):
        for direction in (0, 1):
            step(0, n, block, direction)

    def take_mate_kv(n):
        remote(x_ref.at[both, :, columns(core, n)], kv.at[n, :, rows(other_core)], mate_send.at[0, n], mate_recv.at[0, n], mate).wait_recv()

    start(mate_kv(0))
    give(0, OWN)
    start(mate_kv(1))
    start(mate_q(0))
    start(mate_q(1))
    take_mate_kv(0)
    give(0, MATE)
    relay(0, 0)
    start(far_q(0, FAR))

    get_masks.wait()
    lane = lax.broadcasted_iota(jnp.int32, (TILES, TILES, 2, 128), 3)
    for back in (0, 1, 2):
        who = lax.rem(video + videos - back, videos)
        value = jnp.sum(jnp.where(lane == who, masks[...].astype(jnp.float32), 0.0), axis=3, keepdims=True)
        seen[back] = jnp.broadcast_to(jnp.where(value > 0.5, 0.0, -jnp.inf), (TILES, TILES, 2, 128))
    for t in range(HTILES):
        j = half * HTILES + t
        bias[t] = jnp.zeros((TILES, 128), jnp.float32)
        bias[HTILES + t] = seen[0, :, j, 0, :]
        bias[2 * HTILES + t] = seen[0, :, j, 1, :]
        bias[3 * HTILES + t] = seen[1, j, :, 0, :]
        bias[4 * HTILES + t] = seen[2, j, :, 1, :]
    bias[5 * HTILES] = jnp.full((TILES, 128), -jnp.inf, jnp.float32)
    kv[:, :, pl.ds(5 * HALF, SPAN - 5 * HALF), :] = jnp.zeros((2, 2, SPAN - 5 * HALF, WIDTH), jnp.bfloat16)

    hand_on_early(0)
    start(far_q(0, CROSS))
    give(1, OWN)
    take_mate_kv(1)
    give(1, MATE)
    relay(0, 1)
    hand_on_late(0)
    relay(1, 0)
    start(far_q(1, FAR))
    hand_on_early(1)
    start(far_q(1, CROSS))
    hand_on_late(1)
    relay(1, 1)

    stacked = 2 * HALF

    def attend(index):
        n, local = lax.rem(index, 2), index // 2
        query_tile = jnp.where(local == 1, half, other_half) * HTILES
        for pair in (0, 1):
            lanes = pl.ds(128 * pair, PAIR)
            base = 64 * pair
            at = lax.broadcasted_iota(jnp.int32, (HALF, PAIR), 1)
            qp = q[index, :, lanes]
            heads = [jnp.where((at >= base + DH * m) & (at < base + DH * (m + 1)), qp, jnp.zeros_like(qp)) for m in (0, 1)]
            qs = jnp.concatenate(heads, axis=0)
            top[...] = jnp.full((stacked, 128), -jnp.inf, jnp.float32)

            def score(i, _):
                for kb in (0, 1):
                    at_key = pl.multiple_of(i * (2 * KEYS) + kb * KEYS, KEYS)
                    k = kv[n, 0, pl.ds(at_key, KEYS), lanes]
                    sc = lax.dot_general(qs, k, (((1,), (1,)), ((), ())), preferred_element_type=jnp.float32)
                    cols = []
                    for kt in (0, 1):
                        parts = [jnp.broadcast_to(bias[i * 4 + kb * 2 + kt, pl.ds(query_tile + r, 1), :], (TILE, 128)) for r in range(HTILES)]
                        cols.append(jnp.concatenate(parts * 2, axis=0))
                    sc = sc + jnp.concatenate(cols, axis=1)
                    scores[i * 2 + kb] = sc
                    top[...] = jnp.maximum(top[...], jnp.maximum(sc[:, :128], sc[:, 128:]))
                return 0

            lax.fori_loop(0, STEPS, score, 0)
            top[...] = jnp.broadcast_to(jnp.max(top[...], axis=1, keepdims=True), (stacked, 128))
            total[...] = jnp.zeros((stacked, 128), jnp.float32)
            acc[...] = jnp.zeros((stacked, PAIR), jnp.float32)

            def weigh(i, _):
                ws = []
                highest = jnp.concatenate([top[...]] * 2, axis=1)
                for kb in (0, 1):
                    w = jnp.exp2((scores[i * 2 + kb] - highest) * SCALE)
                    total[...] += w[:, :128] + w[:, 128:]
                    ws.append(w.astype(jnp.bfloat16))
                at_key = pl.multiple_of(i * (2 * KEYS), KEYS)
                acc[...] += jnp.dot(jnp.concatenate(ws, axis=1), kv[n, 1, pl.ds(at_key, 2 * KEYS), lanes],
                                    preferred_element_type=jnp.float32)
                return 0

            lax.fori_loop(0, STEPS, weigh, 0)
            sums = jnp.sum(total[...], axis=1, keepdims=True)
            o = acc[...] / sums
            o = jnp.where(at < base + DH, o[:HALF], o[HALF:])
            first = at[:, :128]
            stats = jnp.zeros((HALF, 128), jnp.float32) if pair == 0 else stat[index]
            for m in (0, 1):
                head = 2 * pair + m
                mine = pl.ds(m * HALF, HALF)
                stats = jnp.where(first == 2 * head, top[mine, :], stats)
                stats = jnp.where(first == 2 * head + 1, sums[m * HALF:(m + 1) * HALF], stats)
            stat[index] = stats

            def put(ref):
                value = o
                if pair == 1:
                    value = jnp.concatenate([
                        jnp.where(first < 64, ref[n, :, pl.ds(128, 128)].astype(jnp.float32), o[:, :128]), o[:, 128:]], axis=1)
                ref[n, :, lanes] = value.astype(ref.dtype)

            pl.when(local == 0)(lambda: put(part))
            pl.when(local == 1)(lambda: put(near))

    def back(n):
        return (remote(part.at[n], partial_in.at[n], back_send.at[0, n], back_recv.at[0, n], far[FAR]),
                remote(stat_out.at[n], stat_in.at[n], back_send.at[1, n], back_recv.at[1, n], far[FAR]))

    def take_far_q(n, which):
        remote(x_ref.at[0, :, columns(core, n)], q.at[n, rows(core_of[which])], far_send.at[n, which], far_recv.at[n, which],
               far[which]).wait_recv()

    def take_mate_q(n):
        remote(x_ref.at[0, :, columns(core, n)], q.at[2 + n, rows(other_core)], mate_send.at[1, n], mate_recv.at[1, n], mate).wait_recv()

    def unit(index, _):
        for n in (0, 1):
            @pl.when(index == n)
            def _():
                own_kv[n].wait()
                for block in (OWN, MATE):
                    for direction in (0, 1):
                        passing(1, n, block, direction).wait_recv()
                take_far_q(n, FAR)
                take_far_q(n, CROSS)

            @pl.when(index == 2 + n)
            def _():
                own_q[n].wait()
                take_mate_q(n)

        attend(index)
        for n in (0, 1):
            @pl.when(index == n)
            def _():
                stat_out[n] = jnp.transpose(stat[n])[:8]
                for copy in back(n):
                    copy.start()

        return 0

    lax.fori_loop(0, 4, unit, 0)

    keep = [pltpu.make_async_copy(fin.at[n, rows(core)], out_ref.at[:, columns(core, n)], local_sem.at[5 + n]) for n in (0, 1)]

    def send_home(n):
        return remote(fin.at[n, rows(other_core)], out_ref.at[:, columns(core, n)], fin_send.at[n], fin_recv.at[n], mate)

    for n in (0, 1):
        for copy in back(n):
            copy.wait_recv()
        theirs = jnp.transpose(jnp.concatenate([stat_in[n], jnp.zeros((120, HALF), jnp.float32)], axis=0))
        ours = stat[2 + n]
        at = lax.broadcasted_iota(jnp.int32, (HALF, WIDTH), 1)
        for head in range(4):
            top_theirs, top_ours = theirs[:, 2 * head:2 * head + 1], ours[:, 2 * head:2 * head + 1]
            highest = jnp.maximum(top_theirs, top_ours)
            by_theirs = theirs[:, 2 * head + 1:2 * head + 2] * jnp.exp2((top_theirs - highest) * SCALE)
            by_ours = ours[:, 2 * head + 1:2 * head + 2] * jnp.exp2((top_ours - highest) * SCALE)
            whole = by_theirs + by_ours
            share_theirs, share_ours = by_theirs / whole, by_ours / whole
            if head == 0:
                all_theirs = jnp.broadcast_to(share_theirs, (HALF, WIDTH))
                all_ours = jnp.broadcast_to(share_ours, (HALF, WIDTH))
            else:
                all_theirs = jnp.where(at >= head * DH, share_theirs, all_theirs)
                all_ours = jnp.where(at >= head * DH, share_ours, all_ours)
        fin[n] = (partial_in[n].astype(jnp.float32) * all_theirs + near[n] * all_ours).astype(jnp.bfloat16)
        send_home(n).start()
        keep[n].start()

    for n in (0, 1):
        remote(fin.at[n, rows(other_core)], out_ref.at[:, columns(other_core, n)], fin_send.at[n], fin_recv.at[n], mate).wait_recv()
        send_home(n).wait_send()
        keep[n].wait()
        for copy in back(n):
            copy.wait_send()
    for copy in copies:
        copy.wait_send()
    for n in (0, 1):
        for block in (OWN, MATE):
            for direction in (0, 1):
                for kind in (0, 1):
                    passing(kind, n, block, direction).wait_send()

    @pl.when(relaying)
    def _():
        for kind in (0, 1):
            for n in (0, 1):
                hop(kind, n).wait_send()


def body(qkv, tile_masks):
    x = jnp.transpose(qkv[0], (1, 0, 2))
    masks = jnp.transpose(tile_masks, (2, 3, 1, 0))
    dma = pltpu.SemaphoreType.DMA
    stacked = 2 * HALF
    out = pl.pallas_call(
        kernel,
        out_shape=jax.ShapeDtypeStruct((ROWS, x.shape[2]), jnp.bfloat16),
        in_specs=[pl.BlockSpec(memory_space=pl.ANY)] * 2,
        out_specs=pl.BlockSpec(memory_space=pl.ANY),
        scratch_shapes=[
            pltpu.VMEM((2, 2, SPAN, WIDTH), jnp.bfloat16),
            pltpu.VMEM((4, HALF, WIDTH), jnp.bfloat16),
            pltpu.VMEM((2, HALF, WIDTH), jnp.bfloat16),
            pltpu.VMEM((2, HALF, WIDTH), jnp.bfloat16),
            pltpu.VMEM((2, HALF, WIDTH), jnp.float32),
            pltpu.VMEM((2, HALF, WIDTH), jnp.bfloat16),
            pltpu.VMEM((4, HALF, 128), jnp.float32),
            pltpu.VMEM((2, 8, HALF), jnp.float32),
            pltpu.VMEM((2, 8, HALF), jnp.float32),
            pltpu.VMEM((2 * STEPS, stacked, KEYS), jnp.float32),
            pltpu.VMEM((stacked, 128), jnp.float32),
            pltpu.VMEM((stacked, 128), jnp.float32),
            pltpu.VMEM((stacked, PAIR), jnp.float32),
            pltpu.VMEM(masks.shape, jnp.int32),
            pltpu.VMEM((3, TILES, TILES, 2, 128), jnp.float32),
            pltpu.VMEM((4 * STEPS, TILES, 128), jnp.float32),
            pltpu.VMEM((2, 2, ROWS, WIDTH), jnp.bfloat16),
            dma((7,)),
            dma((2, 2)), dma((2, 2)),
            dma((2, 2)), dma((2, 2)),
            dma((2, 2, 2)), dma((2, 2, 2)),
            dma((2, 2, 2)), dma((2, 2, 2)),
            dma((2, 2)), dma((2, 2)),
            dma((2, 2)), dma((2, 2)),
            dma((2,)), dma((2,)),
        ],
        compiler_params=pltpu.CompilerParams(collective_id=1, has_side_effects=True, vmem_limit_bytes=48 * 2**20),
        name="orbit_attention",
    )(x, masks)
    return out[None]


def solution(mesh):
    placed = (P("video", "head", None, None), P())
    return jax.shard_map(
        body, mesh=mesh, in_specs=placed, out_specs=P("video", "head", None), check_vma=False
    )
```

```python
import jax
import jax.numpy as jnp
from jax import lax
from jax.experimental import pallas as pl
from jax.experimental.pallas import tpu as pltpu
from jax.sharding import PartitionSpec as P

MESH = pl.DeviceIdType.MESH
DH = 96
TILE = 128
ROWS = 192
HALF = 384
TILES = 6
HTILES = HALF // TILE
WIDTH = 384
PAIR = 256
KEYS = 256
SPAN = 2048
STEPS = 4
SCALE = DH ** (-0.5) * 1.4426950408889634
OWN, MATE = 0, 1
FAR, CROSS = 0, 1
PLANE = 16
SIDE = 4
EDGE = (0, PLANE - 1)


def kernel(x_ref, masks_ref, out_ref, kv, q, part, partial_in, near, fin, stat, stat_out, stat_in, stack, scores, top, total, acc,
           masks, seen, bias, held, landed, local_sem, mate_send, mate_recv, far_send, far_recv, nb_send, nb_recv, fw_send, fw_recv,
           leap_send, hop_send, hop_recv, land_send, land_recv, back_send, back_recv, fin_send, fin_recv):
    video = lax.axis_index("video")
    group = lax.axis_index("head")
    videos = lax.axis_size("video")
    half, core = group // 2, lax.rem(group, 2)
    other_half, other_core = 1 - half, 1 - core
    up = lax.rem(video + 1, videos)
    down = lax.rem(video + videos - 1, videos)
    planes = videos // PLANE
    plane, column = video // PLANE, lax.rem(video, PLANE)
    across, row = column // SIDE, lax.rem(column, SIDE)

    mate = {"video": video, "head": half * 2 + other_core}
    far = ({"video": video, "head": other_half * 2 + core}, {"video": video, "head": other_half * 2 + other_core})

    def along(direction):
        return {"video": (down, up)[direction], "head": group}

    def at_column(level, col):
        return {"video": lax.rem(level + planes, planes) * PLANE + col, "head": group}

    def columns(of_core, n):
        return pl.ds(pl.multiple_of((of_core * 2 + n) * WIDTH, 128), WIDTH)

    def rows(of_core, slot=0):
        return pl.ds(pl.multiple_of(slot * HALF + of_core * ROWS, 64), ROWS)

    both = pl.ds(1, 2)
    core_of = (core, other_core)

    def remote(src, dst, send, recv, to):
        return pltpu.make_async_remote_copy(
            src_ref=src, dst_ref=dst, send_sem=send, recv_sem=recv, device_id=to, device_id_type=MESH)

    copies = []

    def start(copy):
        copy.start()
        copies.append(copy)

    get_masks = pltpu.make_async_copy(masks_ref, masks, local_sem.at[0])
    own_kv = [pltpu.make_async_copy(x_ref.at[both, :, columns(core, n)], kv.at[n, :, rows(core)], local_sem.at[1 + n]) for n in (0, 1)]
    own_q = [pltpu.make_async_copy(x_ref.at[0, :, columns(core, n)], q.at[2 * n + 1, rows(core)], local_sem.at[3 + n]) for n in (0, 1)]
    get_masks.start()
    for copy in own_kv + own_q:
        copy.start()

    barrier = pltpu.get_barrier_semaphore()

    def greet(to):
        pl.semaphore_signal(barrier, inc=1, device_id=to, device_id_type=MESH)

    for to in (*far, mate, along(0), along(1)):
        greet(to)

    upward = row >= SIDE // 2
    outer = (row == 0) | (row == SIDE - 1)
    origin = row + jnp.where(upward, (SIDE - 1) * SIDE, 0)
    leaving = column != origin
    ahead = jnp.where(upward, 1, -1)
    next_plane = at_column(plane + ahead, column)
    sink = at_column(plane, jnp.where(upward, EDGE[0], EDGE[1]))
    pl.when(leaving)(lambda: greet(at_column(plane, origin)))
    greet(at_column(plane - ahead, column))
    for direction in (0, 1):
        @pl.when(column == EDGE[1 - direction])
        def _():
            for place in range(SIDE):
                for line in (2 * direction, 2 * direction + 1):
                    greet(at_column(plane, place * SIDE + line))

    expected = jnp.where(leaving, 7, 6 + SIDE)
    pl.semaphore_wait(barrier, expected)

    def mate_kv(n):
        return remote(x_ref.at[both, :, columns(other_core, n)], kv.at[n, :, rows(core)], mate_send.at[0, n], mate_recv.at[0, n], mate)

    def mate_q(n):
        return remote(x_ref.at[0, :, columns(other_core, n)], q.at[2 * n + 1, rows(core)], mate_send.at[1, n], mate_recv.at[1, n], mate)

    def far_q(n, which, part=None):
        src, dst = x_ref.at[0, :, columns(core_of[which], n)], q.at[2 * n, rows(core)]
        if part is not None:
            src, dst = src.at[pl.ds(part * (ROWS // 2), ROWS // 2)], dst.at[pl.ds(part * (ROWS // 2), ROWS // 2)]
        return remote(src, dst, far_send.at[n, which], far_recv.at[n, which], far[which])

    slots = ((1, 3), (2, 4))

    def source_of(kind, n, block, direction):
        if kind:
            return kv.at[n, :, rows(core_of[block], slots[0][direction])]
        if block == OWN:
            return x_ref.at[both, :, columns(core, n)]
        return kv.at[n, :, rows(other_core)]

    def sems(kind, n, block, direction):
        send, recv = ((nb_send, nb_recv), (fw_send, fw_recv))[kind]
        return send.at[direction, n, block], recv.at[direction, n, block]

    def target_of(kind, n, block, direction):
        return kv.at[n, :, rows(core_of[block], slots[kind][direction])]

    def passing(kind, n, block, direction):
        return remote(source_of(kind, n, block, direction), target_of(kind, n, block, direction),
                      *sems(kind, n, block, direction), along(direction))

    def step(kind, n, block, direction):
        pl.when(column != EDGE[direction])(passing(kind, n, block, direction).start)

    def leap(n, block):
        @pl.when(column == origin)
        def _():
            for which in (0, 1):
                place = block * 2 + which
                src = source_of(0, n, block, 0).at[which]
                pl.when(across == place)(
                    remote(src, landed.at[n], leap_send.at[n, block], land_recv.at[n], next_plane).start)
                pl.when(across != place)(
                    remote(src, held.at[n], leap_send.at[n, block], hop_recv.at[n], at_column(plane, place * SIDE + row)).start)

    def hop(n):
        return remote(held.at[n], landed.at[n], hop_send.at[n], land_recv.at[n], next_plane)

    def land(n, kind):
        block, which = across // 2, lax.rem(across, 2)
        slot = jnp.where(upward, slots[kind][1], slots[kind][0])
        recv = (nb_recv, fw_recv)[kind].at[upward.astype(jnp.int32), n, block]
        return remote(landed.at[n], kv.at[n, which, rows(lax.rem(core + block, 2), slot)], land_send.at[n], recv, sink)

    def relay(n):
        @pl.when(leaving)
        def _():
            remote(held.at[n], held.at[n], hop_send.at[n], hop_recv.at[n], next_plane).wait_recv()
            hop(n).start()

    def arrive(n, kind):
        @pl.when(outer if kind == 0 else jnp.logical_not(outer))
        def _():
            hop(n).wait_recv()
            land(n, kind).start()

    def hand_on(n, direction):
        for block in (OWN, MATE):
            passing(0, n, block, direction).wait_recv()
            step(1, n, block, direction)

    def hand_on_early(n, direction):
        pl.when(column != EDGE[1 - direction])(lambda: hand_on(n, direction))

    def hand_on_late(n):
        for direction in (0, 1):
            pl.when(column == EDGE[1 - direction])(lambda direction=direction: hand_on(n, direction))

    def give(n, block):
        for direction in (0, 1):
            step(0, n, block, direction)

    def take_mate_kv(n):
        remote(x_ref.at[both, :, columns(core, n)], kv.at[n, :, rows(other_core)], mate_send.at[0, n], mate_recv.at[0, n], mate).wait_recv()

    start(mate_kv(0))
    leap(0, OWN)
    give(0, OWN)
    far_q(0, FAR, 0).start()
    start(mate_kv(1))
    start(mate_q(0))
    start(mate_q(1))
    take_mate_kv(0)
    leap(0, MATE)
    give(0, MATE)
    leap(1, OWN)
    take_mate_kv(1)
    leap(1, MATE)
    relay(0)
    relay(1)
    far_q(0, FAR, 1).start()
    copies.append(far_q(0, FAR))

    get_masks.wait()
    lane = lax.broadcasted_iota(jnp.int32, (TILES, TILES, 2, 128), 3)
    for back in (0, 1, 2):
        who = lax.rem(video + videos - back, videos)
        value = jnp.sum(jnp.where(lane == who, masks[...].astype(jnp.float32), 0.0), axis=3, keepdims=True)
        seen[back] = jnp.broadcast_to(jnp.where(value > 0.5, 0.0, -jnp.inf), (TILES, TILES, 2, 128))
    for t in range(HTILES):
        j = half * HTILES + t
        bias[t] = jnp.zeros((TILES, 128), jnp.float32)
        bias[HTILES + t] = seen[0, :, j, 0, :]
        bias[2 * HTILES + t] = seen[0, :, j, 1, :]
        bias[3 * HTILES + t] = seen[1, j, :, 0, :]
        bias[4 * HTILES + t] = seen[2, j, :, 1, :]
    bias[5 * HTILES] = jnp.full((TILES, 128), -jnp.inf, jnp.float32)
    kv[:, :, pl.ds(5 * HALF, SPAN - 5 * HALF), :] = jnp.zeros((2, 2, SPAN - 5 * HALF, WIDTH), jnp.bfloat16)

    start(far_q(0, CROSS))
    hand_on_early(0, 0)
    hand_on_early(0, 1)
    start(far_q(1, FAR))
    arrive(0, 0)
    arrive(0, 1)
    give(1, OWN)
    give(1, MATE)
    start(far_q(1, CROSS))
    hand_on_late(0)
    hand_on_early(1, 0)
    hand_on_early(1, 1)
    arrive(1, 0)

    stacked = 2 * HALF

    def attend(index):
        n, local = index // 2, lax.rem(index, 2)
        query_tile = jnp.where(local == 1, half, other_half) * HTILES
        at = lax.broadcasted_iota(jnp.int32, (HALF, PAIR), 1)
        lanes = [pl.ds(128 * pair, PAIR) for pair in (0, 1)]
        base = (0, 64)
        for pair in (0, 1):
            qp = q[index, :, lanes[pair]]
            for m in (0, 1):
                low = base[pair] + DH * m
                stack[pair, pl.ds(m * HALF, HALF), :] = jnp.where((at >= low) & (at < low + DH), qp, jnp.zeros_like(qp))
            top[pair] = jnp.full((stacked, 128), -jnp.inf, jnp.float32)
            total[pair] = jnp.zeros((stacked, 128), jnp.float32)
            acc[pair] = jnp.zeros((stacked, PAIR), jnp.float32)

        def score(pair, i):
            for kb in (0, 1):
                at_key = pl.multiple_of(i * (2 * KEYS) + kb * KEYS, KEYS)
                k = kv[n, 0, pl.ds(at_key, KEYS), lanes[pair]]
                sc = lax.dot_general(stack[pair], k, (((1,), (1,)), ((), ())), preferred_element_type=jnp.float32)
                cols = []
                for kt in (0, 1):
                    parts = [jnp.broadcast_to(bias[i * 4 + kb * 2 + kt, pl.ds(query_tile + r, 1), :], (TILE, 128)) for r in range(HTILES)]
                    cols.append(jnp.concatenate(parts * 2, axis=0))
                sc = sc + jnp.concatenate(cols, axis=1)
                scores[pair, i * 2 + kb] = sc
                top[pair] = jnp.maximum(top[pair], jnp.maximum(sc[:, :128], sc[:, 128:]))

        def weigh(pair, i):
            ws = []
            highest = jnp.concatenate([top[pair]] * 2, axis=1)
            for kb in (0, 1):
                w = jnp.exp2((scores[pair, i * 2 + kb] - highest) * SCALE)
                total[pair] += w[:, :128] + w[:, 128:]
                ws.append(w.astype(jnp.bfloat16))
            at_key = pl.multiple_of(i * (2 * KEYS), KEYS)
            acc[pair] += jnp.dot(jnp.concatenate(ws, axis=1), kv[n, 1, pl.ds(at_key, 2 * KEYS), lanes[pair]],
                                 preferred_element_type=jnp.float32)

        def highest_of(pair):
            top[pair] = jnp.broadcast_to(jnp.max(top[pair], axis=1, keepdims=True), (stacked, 128))

        def finish(pair):
            sums = jnp.sum(total[pair], axis=1, keepdims=True)
            o = acc[pair] / sums
            o = jnp.where(at < base[pair] + DH, o[:HALF], o[HALF:])
            first = at[:, :128]
            stats = jnp.zeros((HALF, 128), jnp.float32) if pair == 0 else stat[index]
            for m in (0, 1):
                head = 2 * pair + m
                stats = jnp.where(first == 2 * head, top[pair, pl.ds(m * HALF, HALF), :], stats)
                stats = jnp.where(first == 2 * head + 1, sums[m * HALF:(m + 1) * HALF], stats)
            stat[index] = stats

            def put(ref):
                value = o
                if pair == 1:
                    value = jnp.concatenate([
                        jnp.where(first < 64, ref[n, :, pl.ds(128, 128)].astype(jnp.float32), o[:, :128]), o[:, 128:]], axis=1)
                ref[n, :, lanes[pair]] = value.astype(ref.dtype)

            pl.when(local == 0)(lambda: put(part))
            pl.when(local == 1)(lambda: put(near))

        @pl.loop(0, STEPS)
        def _(i):
            score(0, i)

        highest_of(0)

        @pl.loop(0, STEPS)
        def _(i):
            weigh(0, i)
            score(1, i)

        highest_of(1)
        finish(0)

        @pl.loop(0, STEPS)
        def _(i):
            weigh(1, i)

        finish(1)

    def back(n):
        return (remote(part.at[n], partial_in.at[n], back_send.at[0, n], back_recv.at[0, n], far[FAR]),
                remote(stat_out.at[n], stat_in.at[n], back_send.at[1, n], back_recv.at[1, n], far[FAR]))

    def take_far_q(n, which):
        remote(x_ref.at[0, :, columns(core, n)], q.at[2 * n, rows(core_of[which])], far_send.at[n, which], far_recv.at[n, which],
               far[which]).wait_recv()

    def take_mate_q(n):
        remote(x_ref.at[0, :, columns(core, n)], q.at[2 * n + 1, rows(other_core)], mate_send.at[1, n], mate_recv.at[1, n], mate).wait_recv()

    def unit(index, _):
        for n in (0, 1):
            @pl.when(index == 2 * n)
            def _():
                own_kv[n].wait()
                for block in (OWN, MATE):
                    for direction in (0, 1):
                        passing(1, n, block, direction).wait_recv()
                take_far_q(n, FAR)
                take_far_q(n, CROSS)

            @pl.when(index == 2 * n + 1)
            def _():
                own_q[n].wait()
                take_mate_q(n)

        attend(index)
        for n in (0, 1):
            @pl.when(index == 2 * n)
            def _():
                stat_out[n] = jnp.transpose(stat[2 * n])[:8]
                for copy in back(n):
                    copy.start()
                if n == 0:
                    hand_on_late(1)
                    arrive(1, 1)

        return 0

    lax.fori_loop(0, 4, unit, 0)

    keep = [pltpu.make_async_copy(fin.at[n, rows(core)], out_ref.at[:, columns(core, n)], local_sem.at[5 + n]) for n in (0, 1)]

    def send_home(n):
        return remote(fin.at[n, rows(other_core)], out_ref.at[:, columns(core, n)], fin_send.at[n], fin_recv.at[n], mate)

    for n in (0, 1):
        for copy in back(n):
            copy.wait_recv()
        theirs = jnp.transpose(jnp.concatenate([stat_in[n], jnp.zeros((120, HALF), jnp.float32)], axis=0))
        ours = stat[2 * n + 1]
        at = lax.broadcasted_iota(jnp.int32, (HALF, WIDTH), 1)
        for head in range(4):
            top_theirs, top_ours = theirs[:, 2 * head:2 * head + 1], ours[:, 2 * head:2 * head + 1]
            highest = jnp.maximum(top_theirs, top_ours)
            by_theirs = theirs[:, 2 * head + 1:2 * head + 2] * jnp.exp2((top_theirs - highest) * SCALE)
            by_ours = ours[:, 2 * head + 1:2 * head + 2] * jnp.exp2((top_ours - highest) * SCALE)
            whole = by_theirs + by_ours
            share_theirs, share_ours = by_theirs / whole, by_ours / whole
            if head == 0:
                all_theirs = jnp.broadcast_to(share_theirs, (HALF, WIDTH))
                all_ours = jnp.broadcast_to(share_ours, (HALF, WIDTH))
            else:
                all_theirs = jnp.where(at >= head * DH, share_theirs, all_theirs)
                all_ours = jnp.where(at >= head * DH, share_ours, all_ours)
        fin[n] = (partial_in[n].astype(jnp.float32) * all_theirs + near[n] * all_ours).astype(jnp.bfloat16)
        send_home(n).start()
        keep[n].start()

    for n in (0, 1):
        remote(fin.at[n, rows(other_core)], out_ref.at[:, columns(other_core, n)], fin_send.at[n], fin_recv.at[n], mate).wait_recv()
        send_home(n).wait_send()
        keep[n].wait()
        for copy in back(n):
            copy.wait_send()
    for copy in copies:
        copy.wait_send()
    for n in (0, 1):
        for block in (OWN, MATE):
            for direction in (0, 1):
                for kind in (0, 1):
                    pl.when(column != EDGE[direction])(passing(kind, n, block, direction).wait_send)
            pl.when(column == origin)(
                remote(kv.at[n, :, rows(core)], kv.at[n, :, rows(core)], leap_send.at[n, block], nb_recv.at[0, n, block], mate).wait_send)
        pl.when(leaving)(hop(n).wait_send)
        land(n, 0).wait_send()


def body(qkv, tile_masks):
    x = jnp.transpose(qkv[0], (1, 0, 2))
    masks = jnp.transpose(tile_masks, (2, 3, 1, 0))
    dma = pltpu.SemaphoreType.DMA
    stacked = 2 * HALF
    out = pl.pallas_call(
        kernel,
        out_shape=jax.ShapeDtypeStruct((ROWS, x.shape[2]), jnp.bfloat16),
        in_specs=[pl.BlockSpec(memory_space=pl.ANY)] * 2,
        out_specs=pl.BlockSpec(memory_space=pl.ANY),
        scratch_shapes=[
            pltpu.VMEM((2, 2, SPAN, WIDTH), jnp.bfloat16),
            pltpu.VMEM((4, HALF, WIDTH), jnp.bfloat16),
            pltpu.VMEM((2, HALF, WIDTH), jnp.bfloat16),
            pltpu.VMEM((2, HALF, WIDTH), jnp.bfloat16),
            pltpu.VMEM((2, HALF, WIDTH), jnp.float32),
            pltpu.VMEM((2, HALF, WIDTH), jnp.bfloat16),
            pltpu.VMEM((4, HALF, 128), jnp.float32),
            pltpu.VMEM((2, 8, HALF), jnp.float32),
            pltpu.VMEM((2, 8, HALF), jnp.float32),
            pltpu.VMEM((2, stacked, PAIR), jnp.bfloat16),
            pltpu.VMEM((2, 2 * STEPS, stacked, KEYS), jnp.float32),
            pltpu.VMEM((2, stacked, 128), jnp.float32),
            pltpu.VMEM((2, stacked, 128), jnp.float32),
            pltpu.VMEM((2, stacked, PAIR), jnp.float32),
            pltpu.VMEM(masks.shape, jnp.int32),
            pltpu.VMEM((3, TILES, TILES, 2, 128), jnp.float32),
            pltpu.VMEM((4 * STEPS, TILES, 128), jnp.float32),
            pltpu.VMEM((2, ROWS, WIDTH), jnp.bfloat16),
            pltpu.VMEM((2, ROWS, WIDTH), jnp.bfloat16),
            dma((7,)),
            dma((2, 2)), dma((2, 2)),
            dma((2, 2)), dma((2, 2)),
            dma((2, 2, 2)), dma((2, 2, 2)),
            dma((2, 2, 2)), dma((2, 2, 2)),
            dma((2, 2)),
            dma((2,)), dma((2,)),
            dma((2,)), dma((2,)),
            dma((2, 2)), dma((2, 2)),
            dma((2,)), dma((2,)),
        ],
        compiler_params=pltpu.CompilerParams(collective_id=1, has_side_effects=True, vmem_limit_bytes=60 * 2**20),
        name="orbit_attention",
    )(x, masks)
    return out[None]


def solution(mesh):
    placed = (P("video", "head", None, None), P())
    return jax.shard_map(
        body, mesh=mesh, in_specs=placed, out_specs=P("video", "head", None), check_vma=False
    )
```

```python
import jax
import jax.numpy as jnp
from jax import lax
from jax.experimental import pallas as pl
from jax.experimental.pallas import tpu as pltpu
from jax.sharding import PartitionSpec as P

MESH = pl.DeviceIdType.MESH
DH = 96
TILE = 128
ROWS = 192
HALF = 384
TILES = 6
HTILES = HALF // TILE
WIDTH = 384
PAIR = 256
KEYS = 256
SPAN = 2048
STEPS = 4
SCALE = DH ** (-0.5) * 1.4426950408889634
OWN, MATE = 0, 1
FAR, CROSS = 0, 1
PLANE = 16
SIDE = 4
SLOW = (PLANE - SIDE, SIDE - 1)
EDGE = (0, PLANE - 1)


def kernel(x_ref, masks_ref, out_ref, kv, q, part, partial_in, near, fin, stat, stat_out, stat_in, shares, stack, scores, top, total, acc,
           masks, seen, bias, held, landed, local_sem, mate_send, mate_recv, far_send, far_recv, nb_send, nb_recv, fw_send, fw_recv,
           leap_send, hop_send, hop_recv, land_send, land_recv, back_send, back_recv, fin_send, fin_recv):
    video = lax.axis_index("video")
    group = lax.axis_index("head")
    videos = lax.axis_size("video")
    half, core = group // 2, lax.rem(group, 2)
    other_half, other_core = 1 - half, 1 - core
    up = lax.rem(video + 1, videos)
    down = lax.rem(video + videos - 1, videos)
    planes = videos // PLANE
    plane, column = video // PLANE, lax.rem(video, PLANE)
    across, row = column // SIDE, lax.rem(column, SIDE)

    mate = {"video": video, "head": half * 2 + other_core}
    far = ({"video": video, "head": other_half * 2 + core}, {"video": video, "head": other_half * 2 + other_core})

    def along(direction):
        return {"video": (down, up)[direction], "head": group}

    def at_column(level, col):
        return {"video": lax.rem(level + planes, planes) * PLANE + col, "head": group}

    def columns(of_core, n):
        return pl.ds(pl.multiple_of((of_core * 2 + n) * WIDTH, 128), WIDTH)

    def rows(of_core, slot=0):
        return pl.ds(pl.multiple_of(slot * HALF + of_core * ROWS, 64), ROWS)

    both = pl.ds(1, 2)
    core_of = (core, other_core)

    def remote(src, dst, send, recv, to):
        return pltpu.make_async_remote_copy(
            src_ref=src, dst_ref=dst, send_sem=send, recv_sem=recv, device_id=to, device_id_type=MESH)

    copies = []

    def start(copy):
        copy.start()
        copies.append(copy)

    get_masks = pltpu.make_async_copy(masks_ref, masks, local_sem.at[0])
    own_kv = [pltpu.make_async_copy(x_ref.at[both, :, columns(core, n)], kv.at[n, :, rows(core)], local_sem.at[1 + n]) for n in (0, 1)]
    own_q = [pltpu.make_async_copy(x_ref.at[0, :, columns(core, n)], q.at[2 * n + 1, rows(core)], local_sem.at[3 + n]) for n in (0, 1)]
    get_masks.start()
    for copy in own_kv + own_q:
        copy.start()

    barrier = pltpu.get_barrier_semaphore()

    def greet(to):
        pl.semaphore_signal(barrier, inc=1, device_id=to, device_id_type=MESH)

    for to in (*far, mate, along(0), along(1)):
        greet(to)

    upward = row >= SIDE // 2
    outer = (row == 0) | (row == SIDE - 1)
    origin = row + jnp.where(upward, (SIDE - 1) * SIDE, 0)
    leaving = column != origin
    ahead = jnp.where(upward, 1, -1)
    next_plane = at_column(plane + ahead, column)
    sink = at_column(plane, jnp.where(upward, EDGE[0], EDGE[1]))
    wrapped = jnp.where(upward, plane == 0, plane == planes - 1)
    pl.when(leaving)(lambda: greet(at_column(plane, origin)))
    greet(at_column(plane - ahead, column))
    for direction in (0, 1):
        @pl.when(column == EDGE[1 - direction])
        def _():
            for place in range(SIDE):
                for line in (2 * direction, 2 * direction + 1):
                    greet(at_column(plane, place * SIDE + line))

    expected = jnp.where(leaving, 7, 6 + SIDE)
    pl.semaphore_wait(barrier, expected)

    def mate_kv(n):
        return remote(x_ref.at[both, :, columns(other_core, n)], kv.at[n, :, rows(core)], mate_send.at[0, n], mate_recv.at[0, n], mate)

    def mate_q(n):
        return remote(x_ref.at[0, :, columns(other_core, n)], q.at[2 * n + 1, rows(core)], mate_send.at[1, n], mate_recv.at[1, n], mate)

    def far_q(n, which, part=None):
        src, dst = x_ref.at[0, :, columns(core_of[which], n)], q.at[2 * n, rows(core)]
        if part is not None:
            src, dst = src.at[pl.ds(part * (ROWS // 2), ROWS // 2)], dst.at[pl.ds(part * (ROWS // 2), ROWS // 2)]
        return remote(src, dst, far_send.at[n, which], far_recv.at[n, which], far[which])

    slots = ((1, 3), (2, 4))

    def source_of(kind, n, block, direction):
        if kind:
            return kv.at[n, :, rows(core_of[block], slots[0][direction])]
        if block == OWN:
            return x_ref.at[both, :, columns(core, n)]
        return kv.at[n, :, rows(other_core)]

    def sems(kind, n, block, direction):
        send, recv = ((nb_send, nb_recv), (fw_send, fw_recv))[kind]
        return send.at[direction, n, block], recv.at[direction, n, block]

    def target_of(kind, n, block, direction):
        return kv.at[n, :, rows(core_of[block], slots[kind][direction])]

    def passing(kind, n, block, direction):
        return remote(source_of(kind, n, block, direction), target_of(kind, n, block, direction),
                      *sems(kind, n, block, direction), along(direction))

    def step(kind, n, block, direction):
        pl.when(column != EDGE[direction])(passing(kind, n, block, direction).start)

    def leap(n, block):
        @pl.when(column == origin)
        def _():
            for which in (0, 1):
                place = block * 2 + which
                src = source_of(0, n, block, 0).at[which]
                pl.when(across == place)(
                    remote(src, landed.at[n], leap_send.at[n, block], land_recv.at[n], next_plane).start)
                pl.when(across != place)(
                    remote(src, held.at[n], leap_send.at[n, block], hop_recv.at[n], at_column(plane, place * SIDE + row)).start)

    def hop(n):
        return remote(held.at[n], landed.at[n], hop_send.at[n], land_recv.at[n], next_plane)

    def land(n, kind):
        block, which = across // 2, lax.rem(across, 2)
        slot = jnp.where(upward, slots[kind][1], slots[kind][0])
        recv = (nb_recv, fw_recv)[kind].at[upward.astype(jnp.int32), n, block]
        return remote(landed.at[n], kv.at[n, which, rows(lax.rem(core + block, 2), slot)], land_send.at[n], recv, sink)

    def relay(n):
        @pl.when(leaving)
        def _():
            remote(held.at[n], held.at[n], hop_send.at[n], hop_recv.at[n], next_plane).wait_recv()
            hop(n).start()

    def arrive(n, kind):
        @pl.when(outer if kind == 0 else jnp.logical_not(outer))
        def _():
            hop(n).wait_recv()
            land(n, kind).start()

    def hand_on(n, direction):
        for block in (OWN, MATE):
            passing(0, n, block, direction).wait_recv()
            step(1, n, block, direction)

    def is_late(n, direction):
        late = column == EDGE[1 - direction]
        return late | (column == SLOW[direction]) if n else late

    def hand_on_early(n, direction):
        pl.when(jnp.logical_not(is_late(n, direction)))(lambda: hand_on(n, direction))

    def hand_on_late(n):
        for direction in (0, 1):
            pl.when(is_late(n, direction))(lambda direction=direction: hand_on(n, direction))

    def give(n, block):
        for direction in (0, 1):
            step(0, n, block, direction)

    def take_mate_kv(n):
        remote(x_ref.at[both, :, columns(core, n)], kv.at[n, :, rows(other_core)], mate_send.at[0, n], mate_recv.at[0, n], mate).wait_recv()

    start(mate_kv(0))
    leap(0, OWN)
    give(0, OWN)
    far_q(0, FAR, 0).start()
    start(mate_kv(1))
    start(mate_q(0))
    start(mate_q(1))
    take_mate_kv(0)
    leap(0, MATE)
    give(0, MATE)
    leap(1, OWN)
    take_mate_kv(1)
    leap(1, MATE)
    relay(0)
    relay(1)
    far_q(0, FAR, 1).start()
    copies.append(far_q(0, FAR))

    get_masks.wait()
    lane = lax.broadcasted_iota(jnp.int32, (TILES, TILES, 2, 128), 3)
    for back in (0, 1, 2):
        who = lax.rem(video + videos - back, videos)
        value = jnp.sum(jnp.where(lane == who, masks[...].astype(jnp.float32), 0.0), axis=3, keepdims=True)
        seen[back] = jnp.broadcast_to(jnp.where(value > 0.5, 0.0, -jnp.inf), (TILES, TILES, 2, 128))
    for t in range(HTILES):
        j = half * HTILES + t
        bias[t] = jnp.zeros((TILES, 128), jnp.float32)
        bias[HTILES + t] = seen[0, :, j, 0, :]
        bias[2 * HTILES + t] = seen[0, :, j, 1, :]
        bias[3 * HTILES + t] = seen[1, j, :, 0, :]
        bias[4 * HTILES + t] = seen[2, j, :, 1, :]
    bias[5 * HTILES] = jnp.full((TILES, 128), -jnp.inf, jnp.float32)
    kv[:, :, pl.ds(5 * HALF, SPAN - 5 * HALF), :] = jnp.zeros((2, 2, SPAN - 5 * HALF, WIDTH), jnp.bfloat16)

    start(far_q(0, CROSS))
    hand_on_early(0, 0)
    hand_on_early(0, 1)
    start(far_q(1, FAR))
    arrive(0, 0)
    arrive(0, 1)
    give(1, OWN)
    give(1, MATE)
    start(far_q(1, CROSS))
    hand_on_late(0)
    hand_on_early(1, 0)
    hand_on_early(1, 1)
    pl.when(jnp.logical_not(wrapped))(lambda: arrive(1, 0))

    stacked = 2 * HALF

    def attend(index):
        n, local = index // 2, lax.rem(index, 2)
        query_tile = jnp.where(local == 1, half, other_half) * HTILES
        at = lax.broadcasted_iota(jnp.int32, (HALF, PAIR), 1)
        lanes = [pl.ds(128 * pair, PAIR) for pair in (0, 1)]
        base = (0, 64)
        for pair in (0, 1):
            qp = q[index, :, lanes[pair]]
            for m in (0, 1):
                low = base[pair] + DH * m
                stack[pair, pl.ds(m * HALF, HALF), :] = jnp.where((at >= low) & (at < low + DH), qp, jnp.zeros_like(qp))
            top[pair] = jnp.full((stacked, 128), -jnp.inf, jnp.float32)
            total[pair] = jnp.zeros((stacked, 128), jnp.float32)
            acc[pair] = jnp.zeros((stacked, PAIR), jnp.float32)

        def score(pair, i):
            for kb in (0, 1):
                at_key = pl.multiple_of(i * (2 * KEYS) + kb * KEYS, KEYS)
                k = kv[n, 0, pl.ds(at_key, KEYS), lanes[pair]]
                sc = lax.dot_general(stack[pair], k, (((1,), (1,)), ((), ())), preferred_element_type=jnp.float32)
                cols = []
                for kt in (0, 1):
                    parts = [jnp.broadcast_to(bias[i * 4 + kb * 2 + kt, pl.ds(query_tile + r, 1), :], (TILE, 128)) for r in range(HTILES)]
                    cols.append(jnp.concatenate(parts * 2, axis=0))
                sc = sc + jnp.concatenate(cols, axis=1)
                scores[pair, i * 2 + kb] = sc
                top[pair] = jnp.maximum(top[pair], jnp.maximum(sc[:, :128], sc[:, 128:]))

        def weigh(pair, i):
            ws = []
            highest = jnp.concatenate([top[pair]] * 2, axis=1)
            for kb in (0, 1):
                w = jnp.exp2((scores[pair, i * 2 + kb] - highest) * SCALE)
                total[pair] += w[:, :128] + w[:, 128:]
                ws.append(w.astype(jnp.bfloat16))
            at_key = pl.multiple_of(i * (2 * KEYS), KEYS)
            acc[pair] += jnp.dot(jnp.concatenate(ws, axis=1), kv[n, 1, pl.ds(at_key, 2 * KEYS), lanes[pair]],
                                 preferred_element_type=jnp.float32)

        def highest_of(pair):
            top[pair] = jnp.broadcast_to(jnp.max(top[pair], axis=1, keepdims=True), (stacked, 128))

        def finish(pair):
            sums = jnp.sum(total[pair], axis=1, keepdims=True)
            o = acc[pair] / sums
            o = jnp.where(at < base[pair] + DH, o[:HALF], o[HALF:])
            first = at[:, :128]
            stats = jnp.zeros((HALF, 128), jnp.float32) if pair == 0 else stat[index]
            for m in (0, 1):
                head = 2 * pair + m
                stats = jnp.where(first == 2 * head, top[pair, pl.ds(m * HALF, HALF), :], stats)
                stats = jnp.where(first == 2 * head + 1, sums[m * HALF:(m + 1) * HALF], stats)
            stat[index] = stats

            def put(ref):
                value = o
                if pair == 1:
                    value = jnp.concatenate([
                        jnp.where(first < 64, ref[n, :, pl.ds(128, 128)].astype(jnp.float32), o[:, :128]), o[:, 128:]], axis=1)
                ref[n, :, lanes[pair]] = value.astype(ref.dtype)

            pl.when(local == 0)(lambda: put(part))
            pl.when(local == 1)(lambda: put(near))

        @pl.loop(0, STEPS)
        def _(i):
            score(0, i)

        highest_of(0)

        @pl.loop(0, STEPS)
        def _(i):
            weigh(0, i)
            score(1, i)

        highest_of(1)
        finish(0)

        @pl.loop(0, STEPS)
        def _(i):
            weigh(1, i)

        finish(1)

    def back(n):
        return (remote(part.at[n], partial_in.at[n], back_send.at[0, n], back_recv.at[0, n], far[FAR]),
                remote(stat_out.at[n], stat_in.at[n], back_send.at[1, n], back_recv.at[1, n], far[FAR]))

    def take_far_q(n, which):
        remote(x_ref.at[0, :, columns(core, n)], q.at[2 * n, rows(core_of[which])], far_send.at[n, which], far_recv.at[n, which],
               far[which]).wait_recv()

    def take_mate_q(n):
        remote(x_ref.at[0, :, columns(core, n)], q.at[2 * n + 1, rows(other_core)], mate_send.at[1, n], mate_recv.at[1, n], mate).wait_recv()

    def unit(index, _):
        for n in (0, 1):
            @pl.when(index == 2 * n)
            def _():
                own_kv[n].wait()
                for block in (OWN, MATE):
                    for direction in (0, 1):
                        passing(1, n, block, direction).wait_recv()
                if n == 0:
                    arrive(1, 1)
                take_far_q(n, FAR)
                take_far_q(n, CROSS)

            @pl.when(index == 2 * n + 1)
            def _():
                own_q[n].wait()
                take_mate_q(n)

        attend(index)
        for n in (0, 1):
            @pl.when(index == 2 * n)
            def _():
                stat_out[n] = jnp.transpose(stat[2 * n])[:8]
                for copy in back(n):
                    copy.start()
                if n == 0:
                    pl.when(wrapped)(lambda: arrive(1, 0))
                    hand_on_late(1)

        return 0

    lax.fori_loop(0, 4, unit, 0)

    keep = [pltpu.make_async_copy(fin.at[n, rows(core)], out_ref.at[:, columns(core, n)], local_sem.at[5 + n]) for n in (0, 1)]

    def send_home(n):
        return remote(fin.at[n, rows(other_core)], out_ref.at[:, columns(core, n)], fin_send.at[n], fin_recv.at[n], mate)

    for n in (0, 1):
        for copy in back(n):
            copy.wait_recv()
        shares[...] = jnp.transpose(jnp.concatenate([stat_in[n], jnp.zeros((120, HALF), jnp.float32)], axis=0))
        for whose in (other_core, core):
            block = rows(whose)
            theirs, ours = shares[block, :], stat[2 * n + 1, block, :]
            at = lax.broadcasted_iota(jnp.int32, (ROWS, WIDTH), 1)
            for head in range(4):
                top_theirs, top_ours = theirs[:, 2 * head:2 * head + 1], ours[:, 2 * head:2 * head + 1]
                highest = jnp.maximum(top_theirs, top_ours)
                by_theirs = theirs[:, 2 * head + 1:2 * head + 2] * jnp.exp2((top_theirs - highest) * SCALE)
                by_ours = ours[:, 2 * head + 1:2 * head + 2] * jnp.exp2((top_ours - highest) * SCALE)
                whole = by_theirs + by_ours
                share_theirs, share_ours = by_theirs / whole, by_ours / whole
                if head == 0:
                    all_theirs = jnp.broadcast_to(share_theirs, (ROWS, WIDTH))
                    all_ours = jnp.broadcast_to(share_ours, (ROWS, WIDTH))
                else:
                    all_theirs = jnp.where(at >= head * DH, share_theirs, all_theirs)
                    all_ours = jnp.where(at >= head * DH, share_ours, all_ours)
            fin[n, block, :] = (partial_in[n, block, :].astype(jnp.float32) * all_theirs + near[n, block, :] * all_ours).astype(jnp.bfloat16)
            if whose is other_core:
                send_home(n).start()
        keep[n].start()

    for n in (0, 1):
        remote(fin.at[n, rows(other_core)], out_ref.at[:, columns(other_core, n)], fin_send.at[n], fin_recv.at[n], mate).wait_recv()
        send_home(n).wait_send()
        keep[n].wait()
        for copy in back(n):
            copy.wait_send()
    for copy in copies:
        copy.wait_send()
    for n in (0, 1):
        for block in (OWN, MATE):
            for direction in (0, 1):
                for kind in (0, 1):
                    pl.when(column != EDGE[direction])(passing(kind, n, block, direction).wait_send)
            pl.when(column == origin)(
                remote(kv.at[n, :, rows(core)], kv.at[n, :, rows(core)], leap_send.at[n, block], nb_recv.at[0, n, block], mate).wait_send)
        pl.when(leaving)(hop(n).wait_send)
        land(n, 0).wait_send()


def body(qkv, tile_masks):
    x = jnp.transpose(qkv[0], (1, 0, 2))
    masks = jnp.transpose(tile_masks, (2, 3, 1, 0))
    dma = pltpu.SemaphoreType.DMA
    stacked = 2 * HALF
    out = pl.pallas_call(
        kernel,
        out_shape=jax.ShapeDtypeStruct((ROWS, x.shape[2]), jnp.bfloat16),
        in_specs=[pl.BlockSpec(memory_space=pl.ANY)] * 2,
        out_specs=pl.BlockSpec(memory_space=pl.ANY),
        scratch_shapes=[
            pltpu.VMEM((2, 2, SPAN, WIDTH), jnp.bfloat16),
            pltpu.VMEM((4, HALF, WIDTH), jnp.bfloat16),
            pltpu.VMEM((2, HALF, WIDTH), jnp.bfloat16),
            pltpu.VMEM((2, HALF, WIDTH), jnp.bfloat16),
            pltpu.VMEM((2, HALF, WIDTH), jnp.float32),
            pltpu.VMEM((2, HALF, WIDTH), jnp.bfloat16),
            pltpu.VMEM((4, HALF, 128), jnp.float32),
            pltpu.VMEM((2, 8, HALF), jnp.float32),
            pltpu.VMEM((2, 8, HALF), jnp.float32),
            pltpu.VMEM((HALF, 128), jnp.float32),
            pltpu.VMEM((2, stacked, PAIR), jnp.bfloat16),
            pltpu.VMEM((2, 2 * STEPS, stacked, KEYS), jnp.float32),
            pltpu.VMEM((2, stacked, 128), jnp.float32),
            pltpu.VMEM((2, stacked, 128), jnp.float32),
            pltpu.VMEM((2, stacked, PAIR), jnp.float32),
            pltpu.VMEM(masks.shape, jnp.int32),
            pltpu.VMEM((3, TILES, TILES, 2, 128), jnp.float32),
            pltpu.VMEM((4 * STEPS, TILES, 128), jnp.float32),
            pltpu.VMEM((2, ROWS, WIDTH), jnp.bfloat16),
            pltpu.VMEM((2, ROWS, WIDTH), jnp.bfloat16),
            dma((7,)),
            dma((2, 2)), dma((2, 2)),
            dma((2, 2)), dma((2, 2)),
            dma((2, 2, 2)), dma((2, 2, 2)),
            dma((2, 2, 2)), dma((2, 2, 2)),
            dma((2, 2)),
            dma((2,)), dma((2,)),
            dma((2,)), dma((2,)),
            dma((2, 2)), dma((2, 2)),
            dma((2,)), dma((2,)),
        ],
        compiler_params=pltpu.CompilerParams(collective_id=1, has_side_effects=True, vmem_limit_bytes=60 * 2**20),
        name="orbit_attention",
    )(x, masks)
    return out[None]


def solution(mesh):
    placed = (P("video", "head", None, None), P())
    return jax.shard_map(
        body, mesh=mesh, in_specs=placed, out_specs=P("video", "head", None), check_vma=False
    )
```

```python
import jax
import jax.numpy as jnp
from jax import lax
from jax.experimental import pallas as pl
from jax.experimental.pallas import tpu as pltpu
from jax.sharding import PartitionSpec as P

MESH = pl.DeviceIdType.MESH
DH = 96
TILE = 128
ROWS = 192
HALF = 384
TILES = 6
HTILES = HALF // TILE
WIDTH = 384
PAIR = 256
KEYS = 256
SPAN = 2048
STEPS = 4
SCALE = DH ** (-0.5) * 1.4426950408889634
OWN, MATE = 0, 1
FAR, CROSS = 0, 1
PLANE = 16
SIDE = 4
SLOW = (PLANE - SIDE, SIDE - 1)
EDGE = (0, PLANE - 1)


def kernel(x_ref, masks_ref, out_ref, kv, q, part, partial_in, near, fin, stat, stat_out, stat_in, shares, stack, scores, top, total, acc,
           masks, seen, bias, held, landed, local_sem, mate_send, mate_recv, far_send, far_recv, nb_send, nb_recv, fw_send, fw_recv,
           leap_send, hop_send, hop_recv, land_send, land_recv, back_send, back_recv, fin_send, fin_recv):
    video = lax.axis_index("video")
    group = lax.axis_index("head")
    videos = lax.axis_size("video")
    half, core = group // 2, lax.rem(group, 2)
    other_half, other_core = 1 - half, 1 - core
    up = lax.rem(video + 1, videos)
    down = lax.rem(video + videos - 1, videos)
    planes = videos // PLANE
    plane, column = video // PLANE, lax.rem(video, PLANE)
    across, row = column // SIDE, lax.rem(column, SIDE)

    mate = {"video": video, "head": half * 2 + other_core}
    far = ({"video": video, "head": other_half * 2 + core}, {"video": video, "head": other_half * 2 + other_core})

    def along(direction):
        return {"video": (down, up)[direction], "head": group}

    def at_column(level, col):
        return {"video": lax.rem(level + planes, planes) * PLANE + col, "head": group}

    def columns(of_core, n):
        return pl.ds(pl.multiple_of((of_core * 2 + n) * WIDTH, 128), WIDTH)

    def rows(of_core, slot=0):
        return pl.ds(pl.multiple_of(slot * HALF + of_core * ROWS, 64), ROWS)

    both = pl.ds(1, 2)
    core_of = (core, other_core)

    def remote(src, dst, send, recv, to):
        return pltpu.make_async_remote_copy(
            src_ref=src, dst_ref=dst, send_sem=send, recv_sem=recv, device_id=to, device_id_type=MESH)

    copies = []

    def start(copy):
        copy.start()
        copies.append(copy)

    get_masks = pltpu.make_async_copy(masks_ref, masks, local_sem.at[0])
    own_kv = [pltpu.make_async_copy(x_ref.at[both, :, columns(core, n)], kv.at[n, :, rows(core)], local_sem.at[1 + n]) for n in (0, 1)]
    own_q = [pltpu.make_async_copy(x_ref.at[0, :, columns(core, n)], q.at[2 * n + 1, rows(core)], local_sem.at[3 + n]) for n in (0, 1)]
    get_masks.start()
    for copy in own_kv + own_q:
        copy.start()

    barrier = pltpu.get_barrier_semaphore()

    def greet(to):
        pl.semaphore_signal(barrier, inc=1, device_id=to, device_id_type=MESH)

    for to in (*far, mate, along(0), along(1)):
        greet(to)

    upward = row >= SIDE // 2
    outer = (row == 0) | (row == SIDE - 1)
    origin = row + jnp.where(upward, (SIDE - 1) * SIDE, 0)
    leaving = column != origin
    ahead = jnp.where(upward, 1, -1)
    next_plane = at_column(plane + ahead, column)
    sink = at_column(plane, jnp.where(upward, EDGE[0], EDGE[1]))
    wrapped = jnp.where(upward, plane == 0, plane == planes - 1)
    pl.when(leaving)(lambda: greet(at_column(plane, origin)))
    greet(at_column(plane - ahead, column))
    for direction in (0, 1):
        @pl.when(column == EDGE[1 - direction])
        def _():
            for place in range(SIDE):
                for line in (2 * direction, 2 * direction + 1):
                    greet(at_column(plane, place * SIDE + line))

    expected = jnp.where(leaving, 7, 6 + SIDE)
    pl.semaphore_wait(barrier, expected)

    def mate_kv(n):
        return remote(x_ref.at[both, :, columns(other_core, n)], kv.at[n, :, rows(core)], mate_send.at[0, n], mate_recv.at[0, n], mate)

    def mate_q(n):
        return remote(x_ref.at[0, :, columns(other_core, n)], q.at[2 * n + 1, rows(core)], mate_send.at[1, n], mate_recv.at[1, n], mate)

    def far_q(n, which, part=None):
        src, dst = x_ref.at[0, :, columns(core_of[which], n)], q.at[2 * n, rows(core)]
        if part is not None:
            src, dst = src.at[pl.ds(part * (ROWS // 2), ROWS // 2)], dst.at[pl.ds(part * (ROWS // 2), ROWS // 2)]
        return remote(src, dst, far_send.at[n, which], far_recv.at[n, which], far[which])

    slots = ((1, 3), (2, 4))

    def source_of(kind, n, block, direction):
        if kind:
            return kv.at[n, :, rows(core_of[block], slots[0][direction])]
        if block == OWN:
            return x_ref.at[both, :, columns(core, n)]
        return kv.at[n, :, rows(other_core)]

    def sems(kind, n, block, direction):
        send, recv = ((nb_send, nb_recv), (fw_send, fw_recv))[kind]
        return send.at[direction, n, block], recv.at[direction, n, block]

    def target_of(kind, n, block, direction):
        return kv.at[n, :, rows(core_of[block], slots[kind][direction])]

    def passing(kind, n, block, direction):
        return remote(source_of(kind, n, block, direction), target_of(kind, n, block, direction),
                      *sems(kind, n, block, direction), along(direction))

    def step(kind, n, block, direction):
        pl.when(column != EDGE[direction])(passing(kind, n, block, direction).start)

    def leap(n, block):
        @pl.when(column == origin)
        def _():
            for which in (0, 1):
                place = block * 2 + which
                src = source_of(0, n, block, 0).at[which]
                pl.when(across == place)(
                    remote(src, landed.at[n], leap_send.at[n, block], land_recv.at[n], next_plane).start)
                pl.when(across != place)(
                    remote(src, held.at[n], leap_send.at[n, block], hop_recv.at[n], at_column(plane, place * SIDE + row)).start)

    def hop(n):
        return remote(held.at[n], landed.at[n], hop_send.at[n], land_recv.at[n], next_plane)

    def land(n, kind):
        block, which = across // 2, lax.rem(across, 2)
        slot = jnp.where(upward, slots[kind][1], slots[kind][0])
        recv = (nb_recv, fw_recv)[kind].at[upward.astype(jnp.int32), n, block]
        return remote(landed.at[n], kv.at[n, which, rows(lax.rem(core + block, 2), slot)], land_send.at[n], recv, sink)

    def relay(n):
        @pl.when(leaving)
        def _():
            remote(held.at[n], held.at[n], hop_send.at[n], hop_recv.at[n], next_plane).wait_recv()
            hop(n).start()

    def arrive(n, kind):
        @pl.when(outer if kind == 0 else jnp.logical_not(outer))
        def _():
            hop(n).wait_recv()
            land(n, kind).start()

    def hand_on(n, direction):
        for block in (OWN, MATE):
            passing(0, n, block, direction).wait_recv()
            step(1, n, block, direction)

    def is_late(n, direction):
        late = column == EDGE[1 - direction]
        return late | (column == SLOW[direction]) if n else late

    def hand_on_early(n, direction):
        pl.when(jnp.logical_not(is_late(n, direction)))(lambda: hand_on(n, direction))

    def hand_on_late(n):
        for direction in (0, 1):
            pl.when(is_late(n, direction))(lambda direction=direction: hand_on(n, direction))

    def give(n, block):
        for direction in (0, 1):
            step(0, n, block, direction)

    def take_mate_kv(n):
        remote(x_ref.at[both, :, columns(core, n)], kv.at[n, :, rows(other_core)], mate_send.at[0, n], mate_recv.at[0, n], mate).wait_recv()

    start(mate_kv(0))
    leap(0, OWN)
    give(0, OWN)
    far_q(0, FAR, 0).start()
    start(mate_kv(1))
    start(mate_q(0))
    start(mate_q(1))
    take_mate_kv(0)
    leap(0, MATE)
    give(0, MATE)
    leap(1, OWN)
    take_mate_kv(1)
    leap(1, MATE)
    relay(0)
    relay(1)
    far_q(0, FAR, 1).start()
    copies.append(far_q(0, FAR))

    get_masks.wait()
    lane = lax.broadcasted_iota(jnp.int32, (TILES, TILES, 2, 128), 3)
    for back in (0, 1, 2):
        who = lax.rem(video + videos - back, videos)
        value = jnp.sum(jnp.where(lane == who, masks[...].astype(jnp.float32), 0.0), axis=3, keepdims=True)
        seen[back] = jnp.broadcast_to(jnp.where(value > 0.5, 0.0, -jnp.inf), (TILES, TILES, 2, 128))
    for t in range(HTILES):
        j = half * HTILES + t
        bias[t] = jnp.zeros((TILES, 128), jnp.float32)
        bias[HTILES + t] = seen[0, :, j, 0, :]
        bias[2 * HTILES + t] = seen[0, :, j, 1, :]
        bias[3 * HTILES + t] = seen[1, j, :, 0, :]
        bias[4 * HTILES + t] = seen[2, j, :, 1, :]
    bias[5 * HTILES] = jnp.full((TILES, 128), -jnp.inf, jnp.float32)
    kv[:, :, pl.ds(5 * HALF, SPAN - 5 * HALF), :] = jnp.zeros((2, 2, SPAN - 5 * HALF, WIDTH), jnp.bfloat16)

    start(far_q(0, CROSS))
    hand_on_early(0, 0)
    hand_on_early(0, 1)
    at_corner = (column == EDGE[0]) | (column == EDGE[1])
    copies.append(far_q(1, FAR))
    copies.append(far_q(1, CROSS))
    far_q(1, FAR, 0).start()
    pl.when(outer)(far_q(1, FAR, 1).start)
    arrive(0, 0)
    arrive(0, 1)
    give(1, OWN)
    give(1, MATE)
    pl.when(at_corner)(far_q(1, CROSS).start)
    hand_on_late(0)
    hand_on_early(1, 0)
    pl.when(jnp.logical_not(outer))(far_q(1, FAR, 1).start)
    pl.when(jnp.logical_not(at_corner))(far_q(1, CROSS).start)
    hand_on_early(1, 1)
    pl.when(jnp.logical_not(wrapped))(lambda: arrive(1, 0))

    stacked = 2 * HALF

    def attend(index):
        n, local = index // 2, lax.rem(index, 2)
        query_tile = jnp.where(local == 1, half, other_half) * HTILES
        at = lax.broadcasted_iota(jnp.int32, (HALF, PAIR), 1)
        lanes = [pl.ds(128 * pair, PAIR) for pair in (0, 1)]
        base = (0, 64)
        for pair in (0, 1):
            qp = q[index, :, lanes[pair]]
            for m in (0, 1):
                low = base[pair] + DH * m
                stack[pair, pl.ds(m * HALF, HALF), :] = jnp.where((at >= low) & (at < low + DH), qp, jnp.zeros_like(qp))
            top[pair] = jnp.full((stacked, 128), -jnp.inf, jnp.float32)
            total[pair] = jnp.zeros((stacked, 128), jnp.float32)
            acc[pair] = jnp.zeros((stacked, PAIR), jnp.float32)

        def score(pair, i):
            for kb in (0, 1):
                at_key = pl.multiple_of(i * (2 * KEYS) + kb * KEYS, KEYS)
                k = kv[n, 0, pl.ds(at_key, KEYS), lanes[pair]]
                sc = lax.dot_general(stack[pair], k, (((1,), (1,)), ((), ())), preferred_element_type=jnp.float32)
                cols = []
                for kt in (0, 1):
                    parts = [jnp.broadcast_to(bias[i * 4 + kb * 2 + kt, pl.ds(query_tile + r, 1), :], (TILE, 128)) for r in range(HTILES)]
                    cols.append(jnp.concatenate(parts * 2, axis=0))
                sc = sc + jnp.concatenate(cols, axis=1)
                scores[pair, i * 2 + kb] = sc
                top[pair] = jnp.maximum(top[pair], jnp.maximum(sc[:, :128], sc[:, 128:]))

        def weigh(pair, i):
            ws = []
            highest = jnp.concatenate([top[pair]] * 2, axis=1)
            for kb in (0, 1):
                w = jnp.exp2((scores[pair, i * 2 + kb] - highest) * SCALE)
                total[pair] += w[:, :128] + w[:, 128:]
                ws.append(w.astype(jnp.bfloat16))
            at_key = pl.multiple_of(i * (2 * KEYS), KEYS)
            acc[pair] += jnp.dot(jnp.concatenate(ws, axis=1), kv[n, 1, pl.ds(at_key, 2 * KEYS), lanes[pair]],
                                 preferred_element_type=jnp.float32)

        def highest_of(pair):
            top[pair] = jnp.broadcast_to(jnp.max(top[pair], axis=1, keepdims=True), (stacked, 128))

        def finish(pair):
            sums = jnp.sum(total[pair], axis=1, keepdims=True)
            o = acc[pair] / sums
            o = jnp.where(at < base[pair] + DH, o[:HALF], o[HALF:])
            first = at[:, :128]
            stats = jnp.zeros((HALF, 128), jnp.float32) if pair == 0 else stat[index]
            for m in (0, 1):
                head = 2 * pair + m
                stats = jnp.where(first == 2 * head, top[pair, pl.ds(m * HALF, HALF), :], stats)
                stats = jnp.where(first == 2 * head + 1, sums[m * HALF:(m + 1) * HALF], stats)
            stat[index] = stats

            def put(ref):
                value = o
                if pair == 1:
                    value = jnp.concatenate([
                        jnp.where(first < 64, ref[n, :, pl.ds(128, 128)].astype(jnp.float32), o[:, :128]), o[:, 128:]], axis=1)
                ref[n, :, lanes[pair]] = value.astype(ref.dtype)

            pl.when(local == 0)(lambda: put(part))
            pl.when(local == 1)(lambda: put(near))

        @pl.loop(0, STEPS)
        def _(i):
            score(0, i)

        highest_of(0)

        @pl.loop(0, STEPS)
        def _(i):
            weigh(0, i)
            score(1, i)

        highest_of(1)
        finish(0)

        @pl.loop(0, STEPS)
        def _(i):
            weigh(1, i)

        finish(1)

    def back(n):
        return (remote(part.at[n], partial_in.at[n], back_send.at[0, n], back_recv.at[0, n], far[FAR]),
                remote(stat_out.at[n], stat_in.at[n], back_send.at[1, n], back_recv.at[1, n], far[FAR]))

    def take_far_q(n, which):
        remote(x_ref.at[0, :, columns(core, n)], q.at[2 * n, rows(core_of[which])], far_send.at[n, which], far_recv.at[n, which],
               far[which]).wait_recv()

    def take_mate_q(n):
        remote(x_ref.at[0, :, columns(core, n)], q.at[2 * n + 1, rows(other_core)], mate_send.at[1, n], mate_recv.at[1, n], mate).wait_recv()

    def unit(index, _):
        for n in (0, 1):
            @pl.when(index == 2 * n)
            def _():
                own_kv[n].wait()
                for block in (OWN, MATE):
                    for direction in (0, 1):
                        passing(1, n, block, direction).wait_recv()
                if n == 0:
                    arrive(1, 1)
                take_far_q(n, FAR)
                take_far_q(n, CROSS)

            @pl.when(index == 2 * n + 1)
            def _():
                own_q[n].wait()
                take_mate_q(n)

        attend(index)
        for n in (0, 1):
            @pl.when(index == 2 * n)
            def _():
                stat_out[n] = jnp.transpose(stat[2 * n])[:8]
                for copy in back(n):
                    copy.start()
                if n == 0:
                    pl.when(wrapped)(lambda: arrive(1, 0))
                    hand_on_late(1)

        return 0

    lax.fori_loop(0, 4, unit, 0)

    keep = [pltpu.make_async_copy(fin.at[n, rows(core)], out_ref.at[:, columns(core, n)], local_sem.at[5 + n]) for n in (0, 1)]

    def send_home(n):
        return remote(fin.at[n, rows(other_core)], out_ref.at[:, columns(core, n)], fin_send.at[n], fin_recv.at[n], mate)

    for n in (0, 1):
        for copy in back(n):
            copy.wait_recv()
        shares[...] = jnp.transpose(jnp.concatenate([stat_in[n], jnp.zeros((120, HALF), jnp.float32)], axis=0))
        for whose in (other_core, core):
            block = rows(whose)
            theirs, ours = shares[block, :], stat[2 * n + 1, block, :]
            at = lax.broadcasted_iota(jnp.int32, (ROWS, WIDTH), 1)
            for head in range(4):
                top_theirs, top_ours = theirs[:, 2 * head:2 * head + 1], ours[:, 2 * head:2 * head + 1]
                highest = jnp.maximum(top_theirs, top_ours)
                by_theirs = theirs[:, 2 * head + 1:2 * head + 2] * jnp.exp2((top_theirs - highest) * SCALE)
                by_ours = ours[:, 2 * head + 1:2 * head + 2] * jnp.exp2((top_ours - highest) * SCALE)
                whole = by_theirs + by_ours
                share_theirs, share_ours = by_theirs / whole, by_ours / whole
                if head == 0:
                    all_theirs = jnp.broadcast_to(share_theirs, (ROWS, WIDTH))
                    all_ours = jnp.broadcast_to(share_ours, (ROWS, WIDTH))
                else:
                    all_theirs = jnp.where(at >= head * DH, share_theirs, all_theirs)
                    all_ours = jnp.where(at >= head * DH, share_ours, all_ours)
            fin[n, block, :] = (partial_in[n, block, :].astype(jnp.float32) * all_theirs + near[n, block, :] * all_ours).astype(jnp.bfloat16)
            if whose is other_core:
                send_home(n).start()
        keep[n].start()

    for n in (0, 1):
        remote(fin.at[n, rows(other_core)], out_ref.at[:, columns(other_core, n)], fin_send.at[n], fin_recv.at[n], mate).wait_recv()
        send_home(n).wait_send()
        keep[n].wait()
        for copy in back(n):
            copy.wait_send()
    for copy in copies:
        copy.wait_send()
    for n in (0, 1):
        for block in (OWN, MATE):
            for direction in (0, 1):
                for kind in (0, 1):
                    pl.when(column != EDGE[direction])(passing(kind, n, block, direction).wait_send)
            pl.when(column == origin)(
                remote(kv.at[n, :, rows(core)], kv.at[n, :, rows(core)], leap_send.at[n, block], nb_recv.at[0, n, block], mate).wait_send)
        pl.when(leaving)(hop(n).wait_send)
        land(n, 0).wait_send()


def body(qkv, tile_masks):
    x = jnp.transpose(qkv[0], (1, 0, 2))
    masks = jnp.transpose(tile_masks, (2, 3, 1, 0))
    dma = pltpu.SemaphoreType.DMA
    stacked = 2 * HALF
    out = pl.pallas_call(
        kernel,
        out_shape=jax.ShapeDtypeStruct((ROWS, x.shape[2]), jnp.bfloat16),
        in_specs=[pl.BlockSpec(memory_space=pl.ANY)] * 2,
        out_specs=pl.BlockSpec(memory_space=pl.ANY),
        scratch_shapes=[
            pltpu.VMEM((2, 2, SPAN, WIDTH), jnp.bfloat16),
            pltpu.VMEM((4, HALF, WIDTH), jnp.bfloat16),
            pltpu.VMEM((2, HALF, WIDTH), jnp.bfloat16),
            pltpu.VMEM((2, HALF, WIDTH), jnp.bfloat16),
            pltpu.VMEM((2, HALF, WIDTH), jnp.float32),
            pltpu.VMEM((2, HALF, WIDTH), jnp.bfloat16),
            pltpu.VMEM((4, HALF, 128), jnp.float32),
            pltpu.VMEM((2, 8, HALF), jnp.float32),
            pltpu.VMEM((2, 8, HALF), jnp.float32),
            pltpu.VMEM((HALF, 128), jnp.float32),
            pltpu.VMEM((2, stacked, PAIR), jnp.bfloat16),
            pltpu.VMEM((2, 2 * STEPS, stacked, KEYS), jnp.float32),
            pltpu.VMEM((2, stacked, 128), jnp.float32),
            pltpu.VMEM((2, stacked, 128), jnp.float32),
            pltpu.VMEM((2, stacked, PAIR), jnp.float32),
            pltpu.VMEM(masks.shape, jnp.int32),
            pltpu.VMEM((3, TILES, TILES, 2, 128), jnp.float32),
            pltpu.VMEM((4 * STEPS, TILES, 128), jnp.float32),
            pltpu.VMEM((2, ROWS, WIDTH), jnp.bfloat16),
            pltpu.VMEM((2, ROWS, WIDTH), jnp.bfloat16),
            dma((7,)),
            dma((2, 2)), dma((2, 2)),
            dma((2, 2)), dma((2, 2)),
            dma((2, 2, 2)), dma((2, 2, 2)),
            dma((2, 2, 2)), dma((2, 2, 2)),
            dma((2, 2)),
            dma((2,)), dma((2,)),
            dma((2,)), dma((2,)),
            dma((2, 2)), dma((2, 2)),
            dma((2,)), dma((2,)),
        ],
        compiler_params=pltpu.CompilerParams(collective_id=1, has_side_effects=True, vmem_limit_bytes=60 * 2**20),
        name="orbit_attention",
    )(x, masks)
    return out[None]


def solution(mesh):
    placed = (P("video", "head", None, None), P())
    return jax.shard_map(
        body, mesh=mesh, in_specs=placed, out_specs=P("video", "head", None), check_vma=False
    )
```

```python
import jax
import jax.numpy as jnp
from jax import lax
from jax.experimental import pallas as pl
from jax.experimental.pallas import tpu as pltpu
from jax.sharding import PartitionSpec as P

MESH = pl.DeviceIdType.MESH
DH = 96
TILE = 128
ROWS = 192
HALF = 384
TILES = 6
HTILES = HALF // TILE
WIDTH = 384
PAIR = 256
KEYS = 256
SPAN = 2048
STEPS = 4
SCALE = DH ** (-0.5) * 1.4426950408889634
OWN, MATE = 0, 1
FAR, CROSS = 0, 1
PLANE = 16
SIDE = 4
SLOW = (PLANE - SIDE, SIDE - 1)
EDGE = (0, PLANE - 1)


def kernel(x_ref, masks_ref, out_ref, kv, q, part, partial_in, near, fin, stat, stat_out, stat_in, shares, stack, scores, top, total, acc,
           masks, seen, bias, held, landed, local_sem, mate_send, mate_recv, far_send, far_recv, nb_send, nb_recv, fw_send, fw_recv,
           leap_send, hop_send, hop_recv, land_send, land_recv, back_send, back_recv, fin_send, fin_recv):
    video = lax.axis_index("video")
    group = lax.axis_index("head")
    videos = lax.axis_size("video")
    half, core = group // 2, lax.rem(group, 2)
    other_half, other_core = 1 - half, 1 - core
    up = lax.rem(video + 1, videos)
    down = lax.rem(video + videos - 1, videos)
    planes = videos // PLANE
    plane, column = video // PLANE, lax.rem(video, PLANE)
    across, row = column // SIDE, lax.rem(column, SIDE)

    mate = {"video": video, "head": half * 2 + other_core}
    far = ({"video": video, "head": other_half * 2 + core}, {"video": video, "head": other_half * 2 + other_core})

    def along(direction):
        return {"video": (down, up)[direction], "head": group}

    def at_column(level, col):
        return {"video": lax.rem(level + planes, planes) * PLANE + col, "head": group}

    def columns(of_core, n):
        return pl.ds(pl.multiple_of((of_core * 2 + n) * WIDTH, 128), WIDTH)

    def rows(of_core, slot=0):
        return pl.ds(pl.multiple_of(slot * HALF + of_core * ROWS, 64), ROWS)

    both = pl.ds(1, 2)
    core_of = (core, other_core)

    def remote(src, dst, send, recv, to):
        return pltpu.make_async_remote_copy(
            src_ref=src, dst_ref=dst, send_sem=send, recv_sem=recv, device_id=to, device_id_type=MESH)

    copies = []

    def start(copy):
        copy.start()
        copies.append(copy)

    get_masks = pltpu.make_async_copy(masks_ref, masks, local_sem.at[0])
    own_kv = [pltpu.make_async_copy(x_ref.at[both, :, columns(core, n)], kv.at[n, :, rows(core)], local_sem.at[1 + n]) for n in (0, 1)]
    own_q = [pltpu.make_async_copy(x_ref.at[0, :, columns(core, n)], q.at[2 * n + 1, rows(core)], local_sem.at[3 + n]) for n in (0, 1)]
    get_masks.start()
    for copy in own_kv + own_q:
        copy.start()

    barrier = pltpu.get_barrier_semaphore()

    def greet(to):
        pl.semaphore_signal(barrier, inc=1, device_id=to, device_id_type=MESH)

    for to in (*far, mate, along(0), along(1)):
        greet(to)

    upward = row >= SIDE // 2
    outer = (row == 0) | (row == SIDE - 1)
    origin = row + jnp.where(upward, (SIDE - 1) * SIDE, 0)
    leaving = column != origin
    ahead = jnp.where(upward, 1, -1)
    next_plane = at_column(plane + ahead, column)
    sink = at_column(plane, jnp.where(upward, EDGE[0], EDGE[1]))
    pl.when(leaving)(lambda: greet(at_column(plane, origin)))
    greet(at_column(plane - ahead, column))
    for direction in (0, 1):
        @pl.when(column == EDGE[1 - direction])
        def _():
            for place in range(SIDE):
                for line in (2 * direction, 2 * direction + 1):
                    greet(at_column(plane, place * SIDE + line))

    expected = jnp.where(leaving, 7, 6 + SIDE)
    pl.semaphore_wait(barrier, expected)

    def mate_kv(n):
        return remote(x_ref.at[both, :, columns(other_core, n)], kv.at[n, :, rows(core)], mate_send.at[0, n], mate_recv.at[0, n], mate)

    def mate_q(n):
        return remote(x_ref.at[0, :, columns(other_core, n)], q.at[2 * n + 1, rows(core)], mate_send.at[1, n], mate_recv.at[1, n], mate)

    def far_q(n, which, part=None):
        src, dst = x_ref.at[0, :, columns(core_of[which], n)], q.at[2 * n, rows(core)]
        if part is not None:
            src, dst = src.at[pl.ds(part * (ROWS // 2), ROWS // 2)], dst.at[pl.ds(part * (ROWS // 2), ROWS // 2)]
        return remote(src, dst, far_send.at[n, which], far_recv.at[n, which], far[which])

    slots = ((1, 3), (2, 4))

    def source_of(kind, n, block, direction):
        if kind:
            return kv.at[n, :, rows(core_of[block], slots[0][direction])]
        if block == OWN:
            return x_ref.at[both, :, columns(core, n)]
        return kv.at[n, :, rows(other_core)]

    def sems(kind, n, block, direction):
        send, recv = ((nb_send, nb_recv), (fw_send, fw_recv))[kind]
        return send.at[direction, n, block], recv.at[direction, n, block]

    def target_of(kind, n, block, direction):
        return kv.at[n, :, rows(core_of[block], slots[kind][direction])]

    def passing(kind, n, block, direction):
        return remote(source_of(kind, n, block, direction), target_of(kind, n, block, direction),
                      *sems(kind, n, block, direction), along(direction))

    def step(kind, n, block, direction):
        pl.when(column != EDGE[direction])(passing(kind, n, block, direction).start)

    def leap(n, block):
        @pl.when(column == origin)
        def _():
            for which in (0, 1):
                place = block * 2 + which
                src = source_of(0, n, block, 0).at[which]
                pl.when(across == place)(
                    remote(src, landed.at[n], leap_send.at[n, block], land_recv.at[n], next_plane).start)
                pl.when(across != place)(
                    remote(src, held.at[n], leap_send.at[n, block], hop_recv.at[n], at_column(plane, place * SIDE + row)).start)

    def hop(n):
        return remote(held.at[n], landed.at[n], hop_send.at[n], land_recv.at[n], next_plane)

    def land(n, kind):
        block, which = across // 2, lax.rem(across, 2)
        slot = jnp.where(upward, slots[kind][1], slots[kind][0])
        recv = (nb_recv, fw_recv)[kind].at[upward.astype(jnp.int32), n, block]
        return remote(landed.at[n], kv.at[n, which, rows(lax.rem(core + block, 2), slot)], land_send.at[n], recv, sink)

    def relay(n):
        @pl.when(leaving)
        def _():
            remote(held.at[n], held.at[n], hop_send.at[n], hop_recv.at[n], next_plane).wait_recv()
            hop(n).start()

    def arrive(n, kind):
        @pl.when(outer if kind == 0 else jnp.logical_not(outer))
        def _():
            hop(n).wait_recv()
            land(n, kind).start()

    def hand_on(n, direction):
        for block in (OWN, MATE):
            passing(0, n, block, direction).wait_recv()
            step(1, n, block, direction)

    def is_late(n, direction):
        late = column == EDGE[1 - direction]
        return late | (column == SLOW[direction]) if n else late

    def hand_on_early(n, direction):
        pl.when(jnp.logical_not(is_late(n, direction)))(lambda: hand_on(n, direction))

    def hand_on_late(n):
        for direction in (0, 1):
            pl.when(is_late(n, direction))(lambda direction=direction: hand_on(n, direction))

    def give(n, block):
        for direction in (0, 1):
            step(0, n, block, direction)

    def take_mate_kv(n):
        remote(x_ref.at[both, :, columns(core, n)], kv.at[n, :, rows(other_core)], mate_send.at[0, n], mate_recv.at[0, n], mate).wait_recv()

    start(mate_kv(0))
    leap(0, OWN)
    give(0, OWN)
    far_q(0, FAR, 0).start()
    start(mate_kv(1))
    start(mate_q(0))
    start(mate_q(1))
    take_mate_kv(0)
    leap(0, MATE)
    give(0, MATE)
    leap(1, OWN)
    take_mate_kv(1)
    leap(1, MATE)
    relay(0)
    relay(1)
    far_q(0, FAR, 1).start()
    copies.append(far_q(0, FAR))

    get_masks.wait()
    lane = lax.broadcasted_iota(jnp.int32, (TILES, TILES, 2, 128), 3)
    for back in (0, 1, 2):
        who = lax.rem(video + videos - back, videos)
        value = jnp.sum(jnp.where(lane == who, masks[...].astype(jnp.float32), 0.0), axis=3, keepdims=True)
        seen[back] = jnp.broadcast_to(jnp.where(value > 0.5, 0.0, -jnp.inf), (TILES, TILES, 2, 128))
    for t in range(HTILES):
        j = half * HTILES + t
        bias[t] = jnp.zeros((TILES, 128), jnp.float32)
        bias[HTILES + t] = seen[0, :, j, 0, :]
        bias[2 * HTILES + t] = seen[0, :, j, 1, :]
        bias[3 * HTILES + t] = seen[1, j, :, 0, :]
        bias[4 * HTILES + t] = seen[2, j, :, 1, :]
    bias[5 * HTILES] = jnp.full((TILES, 128), -jnp.inf, jnp.float32)
    kv[:, :, pl.ds(5 * HALF, SPAN - 5 * HALF), :] = jnp.zeros((2, 2, SPAN - 5 * HALF, WIDTH), jnp.bfloat16)

    start(far_q(0, CROSS))
    hand_on_early(0, 0)
    hand_on_early(0, 1)
    start(far_q(1, FAR))
    arrive(0, 0)
    arrive(0, 1)
    give(1, OWN)
    give(1, MATE)
    start(far_q(1, CROSS))
    hand_on_late(0)
    hand_on_early(1, 0)
    hand_on_early(1, 1)
    arrive(1, 0)

    stacked = 2 * HALF

    def attend(index):
        n, local = index // 2, lax.rem(index, 2)
        query_tile = jnp.where(local == 1, half, other_half) * HTILES
        at = lax.broadcasted_iota(jnp.int32, (HALF, PAIR), 1)
        lanes = [pl.ds(128 * pair, PAIR) for pair in (0, 1)]
        base = (0, 64)
        for pair in (0, 1):
            qp = q[index, :, lanes[pair]]
            for m in (0, 1):
                low = base[pair] + DH * m
                stack[pair, pl.ds(m * HALF, HALF), :] = jnp.where((at >= low) & (at < low + DH), qp, jnp.zeros_like(qp))
            top[pair] = jnp.full((stacked, 128), -jnp.inf, jnp.float32)
            total[pair] = jnp.zeros((stacked, 128), jnp.float32)
            acc[pair] = jnp.zeros((stacked, PAIR), jnp.float32)

        def score(pair, i):
            for kb in (0, 1):
                at_key = pl.multiple_of(i * (2 * KEYS) + kb * KEYS, KEYS)
                k = kv[n, 0, pl.ds(at_key, KEYS), lanes[pair]]
                sc = lax.dot_general(stack[pair], k, (((1,), (1,)), ((), ())), preferred_element_type=jnp.float32)
                cols = []
                for kt in (0, 1):
                    parts = [jnp.broadcast_to(bias[i * 4 + kb * 2 + kt, pl.ds(query_tile + r, 1), :], (TILE, 128)) for r in range(HTILES)]
                    cols.append(jnp.concatenate(parts * 2, axis=0))
                sc = sc + jnp.concatenate(cols, axis=1)
                scores[pair, i * 2 + kb] = sc
                top[pair] = jnp.maximum(top[pair], jnp.maximum(sc[:, :128], sc[:, 128:]))

        def weigh(pair, i):
            ws = []
            highest = jnp.concatenate([top[pair]] * 2, axis=1)
            for kb in (0, 1):
                w = jnp.exp2((scores[pair, i * 2 + kb] - highest) * SCALE)
                total[pair] += w[:, :128] + w[:, 128:]
                ws.append(w.astype(jnp.bfloat16))
            at_key = pl.multiple_of(i * (2 * KEYS), KEYS)
            acc[pair] += jnp.dot(jnp.concatenate(ws, axis=1), kv[n, 1, pl.ds(at_key, 2 * KEYS), lanes[pair]],
                                 preferred_element_type=jnp.float32)

        def highest_of(pair):
            top[pair] = jnp.broadcast_to(jnp.max(top[pair], axis=1, keepdims=True), (stacked, 128))

        def finish(pair):
            sums = jnp.sum(total[pair], axis=1, keepdims=True)
            o = acc[pair] / sums
            o = jnp.where(at < base[pair] + DH, o[:HALF], o[HALF:])
            first = at[:, :128]
            stats = jnp.zeros((HALF, 128), jnp.float32) if pair == 0 else stat[index]
            for m in (0, 1):
                head = 2 * pair + m
                stats = jnp.where(first == 2 * head, top[pair, pl.ds(m * HALF, HALF), :], stats)
                stats = jnp.where(first == 2 * head + 1, sums[m * HALF:(m + 1) * HALF], stats)
            stat[index] = stats

            def put(ref):
                value = o
                if pair == 1:
                    value = jnp.concatenate([
                        jnp.where(first < 64, ref[n, :, pl.ds(128, 128)].astype(jnp.float32), o[:, :128]), o[:, 128:]], axis=1)
                ref[n, :, lanes[pair]] = value.astype(ref.dtype)

            pl.when(local == 0)(lambda: put(part))
            pl.when(local == 1)(lambda: put(near))

        @pl.loop(0, STEPS)
        def _(i):
            score(0, i)

        highest_of(0)

        @pl.loop(0, STEPS)
        def _(i):
            weigh(0, i)
            score(1, i)

        highest_of(1)
        finish(0)

        @pl.loop(0, STEPS)
        def _(i):
            weigh(1, i)

        finish(1)

    def back(n):
        return (remote(part.at[n], partial_in.at[n], back_send.at[0, n], back_recv.at[0, n], far[FAR]),
                remote(stat_out.at[n], stat_in.at[n], back_send.at[1, n], back_recv.at[1, n], far[FAR]))

    def take_far_q(n, which):
        remote(x_ref.at[0, :, columns(core, n)], q.at[2 * n, rows(core_of[which])], far_send.at[n, which], far_recv.at[n, which],
               far[which]).wait_recv()

    def take_mate_q(n):
        remote(x_ref.at[0, :, columns(core, n)], q.at[2 * n + 1, rows(other_core)], mate_send.at[1, n], mate_recv.at[1, n], mate).wait_recv()

    def unit(index, _):
        for n in (0, 1):
            @pl.when(index == 2 * n)
            def _():
                own_kv[n].wait()
                for block in (OWN, MATE):
                    for direction in (0, 1):
                        passing(1, n, block, direction).wait_recv()
                take_far_q(n, FAR)
                take_far_q(n, CROSS)

            @pl.when(index == 2 * n + 1)
            def _():
                own_q[n].wait()
                take_mate_q(n)

        attend(index)
        for n in (0, 1):
            @pl.when(index == 2 * n)
            def _():
                stat_out[n] = jnp.transpose(stat[2 * n])[:8]
                for copy in back(n):
                    copy.start()
                if n == 0:
                    hand_on_late(1)
                    arrive(1, 1)

        return 0

    lax.fori_loop(0, 4, unit, 0)

    keep = [pltpu.make_async_copy(fin.at[n, rows(core)], out_ref.at[:, columns(core, n)], local_sem.at[5 + n]) for n in (0, 1)]

    def send_home(n):
        return remote(fin.at[n, rows(other_core)], out_ref.at[:, columns(core, n)], fin_send.at[n], fin_recv.at[n], mate)

    for n in (0, 1):
        for copy in back(n):
            copy.wait_recv()
        shares[...] = jnp.transpose(jnp.concatenate([stat_in[n], jnp.zeros((120, HALF), jnp.float32)], axis=0))
        for whose in (other_core, core):
            block = rows(whose)
            theirs, ours = shares[block, :], stat[2 * n + 1, block, :]
            at = lax.broadcasted_iota(jnp.int32, (ROWS, WIDTH), 1)
            for head in range(4):
                top_theirs, top_ours = theirs[:, 2 * head:2 * head + 1], ours[:, 2 * head:2 * head + 1]
                highest = jnp.maximum(top_theirs, top_ours)
                by_theirs = theirs[:, 2 * head + 1:2 * head + 2] * jnp.exp2((top_theirs - highest) * SCALE)
                by_ours = ours[:, 2 * head + 1:2 * head + 2] * jnp.exp2((top_ours - highest) * SCALE)
                whole = by_theirs + by_ours
                share_theirs, share_ours = by_theirs / whole, by_ours / whole
                if head == 0:
                    all_theirs = jnp.broadcast_to(share_theirs, (ROWS, WIDTH))
                    all_ours = jnp.broadcast_to(share_ours, (ROWS, WIDTH))
                else:
                    all_theirs = jnp.where(at >= head * DH, share_theirs, all_theirs)
                    all_ours = jnp.where(at >= head * DH, share_ours, all_ours)
            fin[n, block, :] = (partial_in[n, block, :].astype(jnp.float32) * all_theirs + near[n, block, :] * all_ours).astype(jnp.bfloat16)
            if whose is other_core:
                send_home(n).start()
        keep[n].start()

    for n in (0, 1):
        remote(fin.at[n, rows(other_core)], out_ref.at[:, columns(other_core, n)], fin_send.at[n], fin_recv.at[n], mate).wait_recv()
        send_home(n).wait_send()
        keep[n].wait()
        for copy in back(n):
            copy.wait_send()
    for copy in copies:
        copy.wait_send()
    for n in (0, 1):
        for block in (OWN, MATE):
            for direction in (0, 1):
                for kind in (0, 1):
                    pl.when(column != EDGE[direction])(passing(kind, n, block, direction).wait_send)
            pl.when(column == origin)(
                remote(kv.at[n, :, rows(core)], kv.at[n, :, rows(core)], leap_send.at[n, block], nb_recv.at[0, n, block], mate).wait_send)
        pl.when(leaving)(hop(n).wait_send)
        land(n, 0).wait_send()


def body(qkv, tile_masks):
    x = jnp.transpose(qkv[0], (1, 0, 2))
    masks = jnp.transpose(tile_masks, (2, 3, 1, 0))
    dma = pltpu.SemaphoreType.DMA
    stacked = 2 * HALF
    out = pl.pallas_call(
        kernel,
        out_shape=jax.ShapeDtypeStruct((ROWS, x.shape[2]), jnp.bfloat16),
        in_specs=[pl.BlockSpec(memory_space=pl.ANY)] * 2,
        out_specs=pl.BlockSpec(memory_space=pl.ANY),
        scratch_shapes=[
            pltpu.VMEM((2, 2, SPAN, WIDTH), jnp.bfloat16),
            pltpu.VMEM((4, HALF, WIDTH), jnp.bfloat16),
            pltpu.VMEM((2, HALF, WIDTH), jnp.bfloat16),
            pltpu.VMEM((2, HALF, WIDTH), jnp.bfloat16),
            pltpu.VMEM((2, HALF, WIDTH), jnp.float32),
            pltpu.VMEM((2, HALF, WIDTH), jnp.bfloat16),
            pltpu.VMEM((4, HALF, 128), jnp.float32),
            pltpu.VMEM((2, 8, HALF), jnp.float32),
            pltpu.VMEM((2, 8, HALF), jnp.float32),
            pltpu.VMEM((HALF, 128), jnp.float32),
            pltpu.VMEM((2, stacked, PAIR), jnp.bfloat16),
            pltpu.VMEM((2, 2 * STEPS, stacked, KEYS), jnp.float32),
            pltpu.VMEM((2, stacked, 128), jnp.float32),
            pltpu.VMEM((2, stacked, 128), jnp.float32),
            pltpu.VMEM((2, stacked, PAIR), jnp.float32),
            pltpu.VMEM(masks.shape, jnp.int32),
            pltpu.VMEM((3, TILES, TILES, 2, 128), jnp.float32),
            pltpu.VMEM((4 * STEPS, TILES, 128), jnp.float32),
            pltpu.VMEM((2, ROWS, WIDTH), jnp.bfloat16),
            pltpu.VMEM((2, ROWS, WIDTH), jnp.bfloat16),
            dma((7,)),
            dma((2, 2)), dma((2, 2)),
            dma((2, 2)), dma((2, 2)),
            dma((2, 2, 2)), dma((2, 2, 2)),
            dma((2, 2, 2)), dma((2, 2, 2)),
            dma((2, 2)),
            dma((2,)), dma((2,)),
            dma((2,)), dma((2,)),
            dma((2, 2)), dma((2, 2)),
            dma((2,)), dma((2,)),
        ],
        compiler_params=pltpu.CompilerParams(collective_id=1, has_side_effects=True, vmem_limit_bytes=60 * 2**20),
        name="orbit_attention",
    )(x, masks)
    return out[None]


def solution(mesh):
    placed = (P("video", "head", None, None), P())
    return jax.shard_map(
        body, mesh=mesh, in_specs=placed, out_specs=P("video", "head", None), check_vma=False
    )
```
